256 devices in a mesh: dp: 8 (over x, core), ctx: 32 (over z, y).
Axes of the slice: x: 4, y: 4, z: 8, core: 2. Of those that a mesh axis runs over, the one named last changes fastest.
Arguments:
- pre_q: bfloat16 [16384, 4096], P(('dp', 'ctx')), may hold values from -6 to 6
- prefix_keys: bfloat16 [16384, 512], P(('dp', 'ctx')), may hold values from -6 to 6
- prefix_values: bfloat16 [16384, 512], P(('dp', 'ctx')), may hold values from -6 to 6
- pre_cot: bfloat16 [16384, 4096], P(('dp', 'ctx')), may hold values from -6 to 6
- gen_q: bfloat16 [16384, 4096], P(('dp', 'ctx')), may hold values from -6 to 6
- rollout_keys: bfloat16 [16384, 512], P(('dp', 'ctx')), may hold values from -6 to 6
- rollout_values: bfloat16 [16384, 512], P(('dp', 'ctx')), may hold values from -6 to 6
- gen_cot: bfloat16 [16384, 4096], P(('dp', 'ctx')), may hold values from -6 to 6
- q_gain: float32 [128], replicated, may hold values from 0.5 to 1.5
- k_gain: float32 [128], replicated, may hold values from 0.5 to 1.5
- piece_dest: int32 [8, 256], P('dp'), may hold values from 0 to 255, as said below
- prefix_parent: int32 [8, 32], P('dp'), may hold values from -1 to 31, as said below
- branch_parent: int32 [8, 32], P('dp'), may hold values from 0 to 31
- rewards: int32 [8, 32], P('dp'), may hold values from 0 to 9
Outputs:
- query_gradient: bfloat16 [32768, 4096], P(('dp', 'ctx'))
- key_gradient: bfloat16 [32768, 512], P(('dp', 'ctx'))
- grad_v: bfloat16 [32768, 512], P(('dp', 'ctx'))
- q_gain_grad: float32 [128], replicated
- k_gain_grad: float32 [128], replicated
The draws below stay inside these ranges and needn't reach their ends.
Inputs may be any that keep to these rules, and one draw needn't show every extreme that they name: `piece_dest`: each row (one group) is a permutation; the pieces of one device go to any one device at most 1 times, and exactly 1 times for some pair. `prefix_parent`: in each row, half of the prefix nodes (rounded down) are roots with -1; every other one names a root of the same row.
All inputs are finite; a program needn't handle non-finite values.
Results may differ from the reference program's by a relative error of at most 0.013.
Values may be sent and summed in bfloat16 or wider, within the bound.
A program may use at most 128 MiB of HBM per device.

```python
import math
import jax
import jax.numpy as jnp
from jax import lax

QUERY_HEADS = 32
KEY_VALUE_HEADS = 4
HEAD_SIZE = 128
NODE_TOKENS = 64
PIECES = 8
BR_DEV = 1
TOK_BR = 64
SEG = 8
MOST = 1
BRANCHES = 32
ROLLOUT_ROWS = 16384
PREFIX_ROW_COUNT = 16384
N_DP = 8
N_CTX = 32


def one_map(key):
    favor_key, score_key, offset_key, slot_key = jax.random.split(key, 4)
    favored = jax.random.randint(favor_key, (), 0, N_CTX).astype(jnp.int32)
    values = jnp.tile(jnp.arange(N_CTX, dtype=jnp.int32), MOST)
    scores = jax.random.permutation(score_key, N_CTX * MOST).astype(jnp.int32)
    scores = jnp.where(values == favored, -1, scores)
    ranked = jnp.argsort(scores, stable=True)
    chosen = values[ranked][:PIECES]
    offsets = jax.random.permutation(offset_key, chosen)
    slot_keys = jax.random.split(slot_key, N_CTX)
    slots = jax.vmap(shuffle_slots)(slot_keys).astype(jnp.int32)
    source = jnp.arange(N_CTX, dtype=jnp.int32)[:, None]
    owner = (source - offsets[slots]) % N_CTX
    return (owner * PIECES + slots).reshape(-1).astype(jnp.int32)


def shuffle_slots(key):
    return jax.random.permutation(key, PIECES)


def draw_piece_dest(key, part):
    key = jax.random.fold_in(key, 11)
    return jax.vmap(one_map)(jax.random.split(key, N_DP))


def one_forest(key):
    order_key, pick_key = jax.random.split(key)
    order = jax.random.permutation(order_key, N_CTX).astype(jnp.int32)
    half = N_CTX // 2
    roots = order[:half]
    picks = jax.random.randint(pick_key, (N_CTX - half,), 0, half)
    values = jnp.concatenate([jnp.full((half,), -1, jnp.int32), roots[picks]])
    return jnp.zeros((N_CTX,), jnp.int32).at[order].set(values)


def draw_prefix_parent(key, part):
    key = jax.random.fold_in(key, 23)
    return jax.vmap(one_forest)(jax.random.split(key, N_DP))


def plant(entries, rng, smallest, high):
    place = [jax.random.randint(jax.random.fold_in(rng, axis), (), 0, length) for axis, length in enumerate(entries.shape)]
    widest = entries.shape.index(max(entries.shape))
    beside = place[:widest] + [(place[widest] + 1) % entries.shape[widest]] + place[widest + 1:]
    return entries.at[tuple(place)].set(smallest).at[tuple(beside)].set(high)


def shard_levels(stream_key, extent, pieces, low, high):
    level = 1.0
    for dim, blocks in pieces:
        heights = jax.random.uniform(jax.random.fold_in(jax.random.fold_in(stream_key, 6), dim), (blocks,), jnp.float32, low / len(pieces), high / len(pieces))
        level = level * jnp.repeat(jnp.exp(heights), extent[dim] // blocks).reshape((-1,) + (1,) * (len(extent) - 1 - dim))
    return level


def noise(own_key, dims, scale, reach, cuts=(), kind=jnp.bfloat16):
    values = scale * jax.random.normal(own_key, dims, jnp.float32)
    if cuts:
        values = values * shard_levels(own_key, dims, cuts, -0.22, 0.18)
    return jnp.clip(values, -reach, reach).astype(kind)


def setup_inputs(seed: int = 0) -> dict:
    seeds = jax.random.split(jax.random.key(seed), 15)
    return {
        "pre_q": noise(seeds[0], (PREFIX_ROW_COUNT, QUERY_HEADS * HEAD_SIZE), 1.0, 6.0, ((0, 256),)),
        "prefix_keys": noise(seeds[1], (PREFIX_ROW_COUNT, KEY_VALUE_HEADS * HEAD_SIZE), 1.0, 6.0, ((0, 256),)),
        "prefix_values": noise(seeds[2], (PREFIX_ROW_COUNT, KEY_VALUE_HEADS * HEAD_SIZE), 1.0, 6.0, ((0, 256),)),
        "pre_cot": noise(seeds[3], (PREFIX_ROW_COUNT, QUERY_HEADS * HEAD_SIZE), 1.0, 6.0, ((0, 256),)),
        "gen_q": noise(seeds[4], (ROLLOUT_ROWS, QUERY_HEADS * HEAD_SIZE), 1.0, 6.0, ((0, 256),)),
        "rollout_keys": noise(seeds[5], (ROLLOUT_ROWS, KEY_VALUE_HEADS * HEAD_SIZE), 1.0, 6.0, ((0, 256),)),
        "rollout_values": noise(seeds[6], (ROLLOUT_ROWS, KEY_VALUE_HEADS * HEAD_SIZE), 1.0, 6.0, ((0, 256),)),
        "gen_cot": noise(seeds[7], (ROLLOUT_ROWS, QUERY_HEADS * HEAD_SIZE), 1.0, 6.0, ((0, 256),)),
        "q_gain": jnp.clip(1.0 + 0.1 * jax.random.normal(seeds[8], (HEAD_SIZE,), jnp.float32), 0.5, 1.5),
        "k_gain": jnp.clip(1.0 + 0.1 * jax.random.normal(seeds[9], (HEAD_SIZE,), jnp.float32), 0.5, 1.5),
        "piece_dest": draw_piece_dest(jax.random.fold_in(seeds[14], 71), 0),
        "prefix_parent": draw_prefix_parent(jax.random.fold_in(seeds[14], 71), 0),
        "branch_parent": plant(jax.random.randint(seeds[12], (N_DP, BRANCHES), 0, N_CTX), jax.random.fold_in(seeds[12], 1), 0, N_CTX - 1).astype(jnp.int32),
        "rewards": plant(jax.random.randint(seeds[13], (N_DP, BRANCHES), 0, 10), jax.random.fold_in(seeds[13], 1), 0, 9).astype(jnp.int32),
    }


EPSILON = 1e-06

def norm_heads(values, gain):
    inverse = lax.rsqrt(lax.optimization_barrier(jnp.mean(values * values, axis=-1, keepdims=True)) + EPSILON)
    return (values * inverse * gain, inverse)

def norm_back(values, inverse, gain, upstream):
    scaled = gain * upstream
    inner = lax.optimization_barrier(jnp.mean(values * scaled, axis=-1, keepdims=True))
    result = inverse * scaled - values * (inverse * inverse * inverse) * inner
    gain_term = lax.optimization_barrier(jnp.sum((upstream * values * inverse).reshape(-1, values.shape[-1]), axis=0))
    return (result, gain_term)

def advantages(rewards_row, prefix_row, branch_row):
    row_count = prefix_row.shape[0]
    match_prefix = branch_row[:, None] == jnp.arange(row_count, dtype=jnp.int32)[None, :]
    upper = lax.optimization_barrier(jnp.sum(jnp.where(match_prefix, prefix_row[None, :], 0), axis=1)).astype(jnp.int32)
    rooted = jnp.where(upper >= 0, upper, branch_row)
    member = (rooted[:, None] == rooted[None, :]).astype(jnp.float32)
    score = rewards_row.astype(jnp.float32)
    sizes = lax.optimization_barrier(jnp.sum(member, axis=1))
    center = lax.optimization_barrier(jnp.sum(member * score[None, :], axis=1)) / sizes
    spread = lax.optimization_barrier(jnp.sum(member * (score[None, :] - center[:, None]) ** 2, axis=1)) / sizes
    return ((score - center) / jnp.maximum(jnp.sqrt(spread), 1.0), upper)

def node_mask(anc_ok, node):
    position = jnp.arange(node, dtype=jnp.int32)
    own = (position[None, :] <= position[:, None]).astype(jnp.float32)
    tree_nodes = anc_ok.shape[0]
    own = jnp.broadcast_to(own, (tree_nodes, node, node))
    far = jnp.broadcast_to(jnp.repeat(anc_ok, node, axis=1)[:, None, :], (tree_nodes, node, 2 * node))
    return jnp.concatenate([own, far], axis=2)[:, None, None]

def attend_grads(query_bfloat, keys_bf, vals_bf, cotangent_bfloat, anc_ok):
    node = query_bfloat.shape[1]
    scale = 1.0 / math.sqrt(query_bfloat.shape[-1])
    flt = jnp.float32
    scores = jnp.einsum('nqcgd,nkcd->ncgqk', query_bfloat.astype(flt), keys_bf.astype(flt)) * scale
    weights = jnp.exp(scores) * node_mask(anc_ok, node)
    probs = weights / lax.optimization_barrier(jnp.sum(weights, axis=-1, keepdims=True))
    probs_bf = probs.astype(jnp.bfloat16)
    dprob = jnp.einsum('nqcgd,nkcd->ncgqk', cotangent_bfloat.astype(flt), vals_bf.astype(flt))
    inner = lax.optimization_barrier(jnp.sum(probs * dprob, axis=-1, keepdims=True))
    dscore_bf = (probs * (dprob - inner) * scale).astype(jnp.bfloat16)
    grad_query = jnp.einsum('ncgqk,nkcd->nqcgd', dscore_bf.astype(flt), keys_bf.astype(flt))
    keys_gradient_total = jnp.einsum('ncgqk,nqcgd->nkcd', dscore_bf.astype(flt), query_bfloat.astype(flt))
    values_gradient = jnp.einsum('ncgqk,nqcgd->nkcd', probs_bf.astype(flt), cotangent_bfloat.astype(flt))
    return (grad_query, keys_gradient_total, values_gradient)

def one_group(pre_q, prefix_keys, prefix_values, pre_cot, gen_q, rollout_keys, rollout_values, gen_cot, q_gain, k_gain, dest, prefix_row, branch_row, rewards_row):
    row_count = N_CTX
    tree_nodes = 1 + BR_DEV
    heads_per_group = QUERY_HEADS // KEY_VALUE_HEADS

    def relay(row_indices):
        width = row_indices.shape[-1]
        parts = row_indices.reshape(row_count * PIECES, SEG, width)
        placed = jnp.zeros_like(parts).at[dest].set(parts)
        return placed.reshape(row_count, BR_DEV, NODE_TOKENS, width)

    def prefix_tree(prefix_rows, branch_rows):
        return jnp.concatenate([prefix_rows.reshape(row_count, 1, NODE_TOKENS, -1), relay(branch_rows)], axis=1)
    q_tree = prefix_tree(pre_q, gen_q).astype(jnp.float32).reshape(row_count, tree_nodes, NODE_TOKENS, QUERY_HEADS, HEAD_SIZE)
    key_tree_order = prefix_tree(prefix_keys, rollout_keys).astype(jnp.float32).reshape(row_count, tree_nodes, NODE_TOKENS, KEY_VALUE_HEADS, HEAD_SIZE)
    value_tree_order = prefix_tree(prefix_values, rollout_values).reshape(row_count, tree_nodes, NODE_TOKENS, KEY_VALUE_HEADS, HEAD_SIZE)
    cotangent_tree = prefix_tree(pre_cot, gen_cot).astype(jnp.float32)
    query_norm, q_inv = norm_heads(q_tree, q_gain)
    k_norm, k_inv = norm_heads(key_tree_order, k_gain)
    query_bfloat = query_norm.astype(jnp.bfloat16).reshape(row_count, tree_nodes, NODE_TOKENS, KEY_VALUE_HEADS, heads_per_group, HEAD_SIZE)
    key_bf = k_norm.astype(jnp.bfloat16)
    adv, upper = advantages(rewards_row, prefix_row, branch_row)
    attention_weight = jnp.concatenate([jnp.ones((row_count, 1), jnp.float32), adv.reshape(row_count, BR_DEV)], axis=1)
    cotangent_bfloat = (attention_weight[:, :, None, None] * cotangent_tree).astype(jnp.bfloat16).reshape(row_count, tree_nodes, NODE_TOKENS, KEY_VALUE_HEADS, heads_per_group, HEAD_SIZE)
    first_ids = jnp.stack([prefix_row, jnp.full((row_count,), -1, jnp.int32)], axis=1)[:, None]
    branch_ids = jnp.stack([branch_row, upper], axis=1).reshape(row_count, BR_DEV, 2)
    anc_ids = jnp.concatenate([first_ids, branch_ids], axis=1).astype(jnp.int32)
    prefix_key_rows = key_bf[:, 0]
    prefix_value_rows = value_tree_order[:, 0]

    def device_step(carry, index):
        ids = anc_ids[index]
        clipped_ratio = jnp.maximum(ids, 0).astype(jnp.int32)
        valid = (ids >= 0).astype(jnp.float32)
        distant_keys = prefix_key_rows[clipped_ratio].reshape(tree_nodes, 2 * NODE_TOKENS, KEY_VALUE_HEADS, HEAD_SIZE)
        distant_values = prefix_value_rows[clipped_ratio].reshape(tree_nodes, 2 * NODE_TOKENS, KEY_VALUE_HEADS, HEAD_SIZE)
        keys = jnp.concatenate([key_bf[index], distant_keys], axis=1)
        vals = jnp.concatenate([value_tree_order[index], distant_values], axis=1)
        grad_query, keys_gradient_total, values_gradient = attend_grads(query_bfloat[index], keys, vals, cotangent_bfloat[index], valid)
        selector = valid[:, :, None, None, None]
        partial_keys = (keys_gradient_total[:, NODE_TOKENS:].reshape(tree_nodes, 2, NODE_TOKENS, KEY_VALUE_HEADS, HEAD_SIZE) * selector).reshape(tree_nodes * 2, NODE_TOKENS, KEY_VALUE_HEADS, HEAD_SIZE)
        partial_values = (values_gradient[:, NODE_TOKENS:].reshape(tree_nodes, 2, NODE_TOKENS, KEY_VALUE_HEADS, HEAD_SIZE) * selector).reshape(tree_nodes * 2, NODE_TOKENS, KEY_VALUE_HEADS, HEAD_SIZE)
        term_key_rows = jnp.zeros((row_count, NODE_TOKENS, KEY_VALUE_HEADS, HEAD_SIZE), jnp.float32).at[clipped_ratio.reshape(-1)].add(partial_keys)
        term_value_rows = jnp.zeros((row_count, NODE_TOKENS, KEY_VALUE_HEADS, HEAD_SIZE), jnp.float32).at[clipped_ratio.reshape(-1)].add(partial_values)
        rounded_k = lax.optimization_barrier(term_key_rows.astype(jnp.bfloat16)).astype(jnp.float32)
        rounded_v = lax.optimization_barrier(term_value_rows.astype(jnp.bfloat16)).astype(jnp.float32)
        return ((carry[0] + rounded_k, carry[1] + rounded_v), (grad_query, keys_gradient_total[:, :NODE_TOKENS], values_gradient[:, :NODE_TOKENS]))
    zero_value = jnp.zeros((row_count, NODE_TOKENS, KEY_VALUE_HEADS, HEAD_SIZE), jnp.float32)
    (far_k, far_v), (grad_qn, grad_kn, value_normed_gradient) = lax.scan(device_step, (zero_value, zero_value), jnp.arange(row_count, dtype=jnp.int32))
    grad_kn = grad_kn.at[:, 0].add(far_k)
    value_normed_gradient = value_normed_gradient.at[:, 0].add(far_v)
    query_gradient, query_norm_term = norm_back(q_tree, q_inv, q_gain, grad_qn.reshape(row_count, tree_nodes, NODE_TOKENS, QUERY_HEADS, HEAD_SIZE))
    key_gradient, key_norm_term = norm_back(key_tree_order, k_inv, k_gain, grad_kn)
    row_indices = row_count * tree_nodes * NODE_TOKENS
    return (query_gradient.reshape(row_indices, QUERY_HEADS * HEAD_SIZE).astype(jnp.bfloat16), key_gradient.reshape(row_indices, KEY_VALUE_HEADS * HEAD_SIZE).astype(jnp.bfloat16), value_normed_gradient.reshape(row_indices, KEY_VALUE_HEADS * HEAD_SIZE).astype(jnp.bfloat16), query_norm_term, key_norm_term)

def reference(pre_q, prefix_keys, prefix_values, pre_cot, gen_q, rollout_keys, rollout_values, gen_cot, q_gain, k_gain, piece_dest, prefix_parent, branch_parent, rewards):
    outs_q, outs_k, outs_v = ([], [], [])
    q_total = jnp.zeros((HEAD_SIZE,), jnp.float32)
    k_total = jnp.zeros((HEAD_SIZE,), jnp.float32)
    pre_rows = N_CTX * NODE_TOKENS
    gen_rows = N_CTX * TOK_BR
    for group in range(N_DP):
        cut_pre = lambda array: array[group * pre_rows:(group + 1) * pre_rows]
        cut_gen = lambda array: array[group * gen_rows:(group + 1) * gen_rows]
        result = one_group(cut_pre(pre_q), cut_pre(prefix_keys), cut_pre(prefix_values), cut_pre(pre_cot), cut_gen(gen_q), cut_gen(rollout_keys), cut_gen(rollout_values), cut_gen(gen_cot), q_gain, k_gain, piece_dest[group], prefix_parent[group], branch_parent[group], rewards[group])
        outs_q.append(result[0])
        outs_k.append(result[1])
        outs_v.append(result[2])
        q_total = q_total + result[3]
        k_total = k_total + result[4]
    return (jnp.concatenate(outs_q, axis=0), jnp.concatenate(outs_k, axis=0), jnp.concatenate(outs_v, axis=0), q_total, k_total)
```

```python
import math

import jax
import jax.numpy as jnp
from jax import lax
from jax.experimental import pallas as pl
from jax.experimental.pallas import tpu as pltpu
from jax.sharding import PartitionSpec as P

EPSILON = 1e-06
NZ, NY = 8, 4
N = NZ * NY
BF = jnp.bfloat16
F32 = jnp.float32
MESH = pl.DeviceIdType.MESH
SCALE = 1.0 / math.sqrt(128)


def iota(shape, axis):
    return lax.broadcasted_iota(jnp.int32, shape, axis)


def contract(a, b, da, db):
    return lax.dot_general(a, b, (((da,), (db,)), ((), ())), preferred_element_type=F32)


def inverse_norm(x):
    return lax.rsqrt(jnp.mean(x * x, axis=-1, keepdims=True) + EPSILON)


def norm_back(x, r, gain, upstream):
    scaled = gain * upstream
    inner = jnp.mean(x * scaled, axis=-1, keepdims=True)
    return r * scaled - x * (r * r * r) * inner


def attend(q, cot, gain, keys, vals, mask):
    r = inverse_norm(q)
    qn = (q * r * gain).astype(BF)
    weights = jnp.exp(contract(keys, qn, 1, 1) * SCALE) * mask
    probs = weights * (1.0 / jnp.sum(weights, axis=0, keepdims=True))
    dprob = contract(vals, cot, 1, 1)
    inner = jnp.sum(probs * dprob, axis=0, keepdims=True)
    dscore = (probs * (dprob - inner) * SCALE).astype(BF)
    dq = contract(dscore, keys, 0, 0)
    dk = contract(dscore, qn, 1, 0)
    dv = contract(probs.astype(BF), cot, 1, 0)
    gain_term = jnp.sum(dq * q * r, axis=0, keepdims=True)
    return norm_back(q, r, gain, dq), dk, dv, gain_term


def kernel(
    pre_q, pre_k, pre_v, pre_c, gen_q, gen_k, gen_v, gen_c, qg, kg,
    dest_row, pp_row, bp_row, rew_row, inv_s, pp_s, bp_s, rew_s,
    out_q, out_k, out_v, out_qg, out_kg,
    kv, r1a, s1b, r1b, s2a, r2a, s2b, r2b, t0, rt0, t12, rt12, s4, r4,
    g, rg, gd, rd, m0, m12, dkp, dvp, causal, send, recv, dsend, drecv,
):
    me = lax.axis_index("ctx")
    group = lax.axis_index("dp")
    n_dp = lax.axis_size("dp")

    def peer(k):
        j = k // NY
        dz = jnp.where(j % 2 == 1, (j + 1) // 2, (NZ - j // 2) % NZ)
        return ((me // NY + dz) % NZ) * NY + (me % NY + k % NY) % NY

    def dp_peer(k):
        return (group + k) % n_dp

    def copy(stage, src, dst, target):
        return pltpu.make_async_remote_copy(
            src_ref=src, dst_ref=dst, send_sem=send.at[stage, target], recv_sem=recv.at[stage, me],
            device_id={"ctx": target}, device_id_type=MESH,
        )

    def await_recv(stage, dst, source):
        pltpu.make_async_copy(dst, dst, recv.at[stage, source]).wait()

    def await_send(stage, src, target):
        pltpu.make_async_copy(src, src, send.at[stage, target]).wait()

    def peers(body):
        @pl.loop(1, N)
        def _(k):
            body(peer(k))

    barrier = pltpu.get_barrier_semaphore()

    @pl.loop(1, N)
    def _(k):
        pl.semaphore_signal(barrier, inc=1, device_id={"ctx": peer(k)}, device_id_type=MESH)

    @pl.loop(1, n_dp)
    def _(k):
        pl.semaphore_signal(barrier, inc=1, device_id={"dp": dp_peer(k)}, device_id_type=MESH)

    kgain = kg[...]
    qgain = qg[...]

    for c in range(4):
        x = pre_k[:, c * 128:(c + 1) * 128].astype(F32)
        kv[0, :, c * 128:(c + 1) * 128] = (x * inverse_norm(x) * kgain).astype(BF)
    kv[0, :, 512:] = pre_v[...]
    rows = iota((64, 64), 0)
    spread = (8 * ((rows % 16) // 2) + 2 * (rows // 16) + rows % 2 == iota((64, 64), 1)).astype(F32).astype(BF)
    kv[1, :, :512] = contract(spread, gen_k[...], 1, 0).astype(BF)
    kv[1, :, 512:] = contract(spread, gen_v[...], 1, 0).astype(BF)

    pl.semaphore_wait(barrier, N - 1 + n_dp - 1)

    def fragment(t):
        rb = pl.multiple_of((t // 8) * 16, 16)
        cb = pl.multiple_of((t % 8) * 128, 128)
        return kv.at[:, pl.ds(rb, 16), pl.ds(cb, 128)]

    def send_1a(t):
        copy(0, fragment(t), r1a.at[me], t).start()

    peers(send_1a)
    r1a[me] = fragment(me)[...]

    def slab(t):
        cols = pl.ds(pl.multiple_of(t * 128, 128), 128)
        q = gen_q[:, cols].astype(F32).reshape(8, 8, 128)
        c = gen_c[:, cols].astype(F32).reshape(8, 8, 128)
        return jnp.concatenate([q, c], axis=1).astype(BF)

    def send_1b(t):
        part = s1b.at[pl.ds(t * 8, 8)]
        part[...] = slab(t)
        copy(1, part, r1b.at[pl.ds(me * 8, 8)], t).start()

    peers(send_1b)
    r1b[pl.ds(me * 8, 8)] = slab(me)

    pp = jnp.broadcast_to(pp_row[...].astype(F32), (8, N))
    bp = jnp.broadcast_to(bp_row[...].astype(F32), (8, N))
    pick = (bp_row[...] == iota((N, N), 0)).astype(F32).astype(BF)
    upper = contract(pp.astype(BF), pick, 1, 0)
    spread0 = (iota((N, 512), 0) == iota((N, 512), 1) // 16).astype(F32).astype(BF)
    row0 = (iota((8, 512), 1) % 16).astype(F32)
    spread1 = (iota((N, 1024), 0) == iota((N, 1024), 1) // 32).astype(F32).astype(BF)
    lane1 = iota((8, 1024), 1)
    id0 = contract(pp.astype(BF), spread0, 1, 0) * 16.0 + row0
    parent1 = contract(bp.astype(BF), spread1, 1, 0)
    upper1 = contract(upper.astype(BF), spread1, 1, 0)
    id1 = jnp.where((lane1 // 16) % 2 == 0, parent1, upper1) * 16.0 + (lane1 % 16).astype(F32)
    m0[...] = (iota((512, 512), 0).astype(F32) == id0[:1]).astype(F32).astype(BF)
    m12[...] = (iota((512, 1024), 0).astype(F32) == id1[:1]).astype(F32).astype(BF)
    dest = jnp.broadcast_to(dest_row[...].astype(F32), (8, 256)).astype(BF)
    spread2 = (iota((256, 512), 0) == iota((256, 512), 1) // 2).astype(F32).astype(BF)
    id2 = contract(dest, spread2, 1, 0) * 2.0 + (iota((8, 512), 1) % 2).astype(F32)
    order = (iota((512, 512), 0).astype(F32) == id2[:1]).astype(F32).astype(BF)
    causal[...] = (iota((64, 512), 0) <= iota((64, 512), 1) % 64).astype(F32)

    my_parent = bp_s[0, me]
    my_upper = pp_s[0, my_parent]
    my_above = pp_s[0, me]
    my_root = jnp.where(my_upper >= 0, my_upper, my_parent).astype(F32)
    root = jnp.where(upper >= 0.0, upper, bp)
    member = (root == my_root).astype(F32)
    score = jnp.broadcast_to(rew_row[...].astype(F32), (8, N))
    size = jnp.sum(member, axis=1, keepdims=True)
    center = jnp.sum(member * score, axis=1, keepdims=True) / size
    var = jnp.sum(member * (score - center) ** 2, axis=1, keepdims=True) / size
    adv = ((rew_s[0, me].astype(F32) - center) / jnp.maximum(jnp.sqrt(var), 1.0))[:1]

    peers(lambda t: await_recv(0, r1a.at[t], t))
    s2a[:, 3] = contract(order, r1a[:, 1].reshape(512, 128), 1, 0).astype(BF).reshape(N, 16, 128)

    def fill_2a(t):
        parent = bp_s[0, t]
        s2a[t, 0] = r1a[jnp.maximum(pp_s[0, t], 0), 0]
        s2a[t, 1] = r1a[parent, 0]
        s2a[t, 2] = r1a[jnp.maximum(pp_s[0, parent], 0), 0]

    def send_2a(t):
        fill_2a(t)
        copy(2, s2a.at[t], r2a.at[me], t).start()

    peers(send_2a)
    fill_2a(me)
    r2a[me] = s2a[me]

    peers(lambda t: await_recv(1, r1b.at[pl.ds(t * 8, 8)], t))

    def send_2b(t):
        for p in range(8):
            s2b[t * 8 + p] = r1b[inv_s[0, t * 8 + p]]
        copy(3, s2b.at[pl.ds(t * 8, 8)], r2b.at[pl.ds(me * 8, 8)], t).start()

    peers(send_2b)
    for p in range(8):
        r2b[me * 8 + p] = r1b[inv_s[0, me * 8 + p]]

    def tiles(ref, at, c):
        return jnp.concatenate([ref[8 * b + c] if at is None else ref[8 * b + c, at] for b in range(4)], axis=0)

    peers(lambda t: await_recv(2, r2a.at[t], t))
    g[...] = jnp.zeros((8, 128), F32)
    above = (my_above >= 0).astype(F32)

    @pl.loop(0, 4)
    def _(c):
        col = lambda base, h: pl.ds(pl.multiple_of((base + h) * 128, 128), 128)
        q = jnp.concatenate([pre_q[:, col(8 * c, h)] for h in range(8)], axis=0).astype(F32)
        cot = jnp.concatenate([pre_c[:, col(8 * c, h)] for h in range(8)], axis=0)
        own_k = kv[0, :, col(c, 0)]
        far_k = tiles(r2a, 0, c)
        keys = jnp.concatenate([own_k, far_k], axis=0)
        vals = jnp.concatenate([kv[0, :, col(c, 4)], tiles(r2a, 0, 4 + c)], axis=0)
        mask = jnp.concatenate([causal[...], jnp.full((64, 512), 1.0, F32) * above], axis=0)
        dq, dk, dv, q_term = attend(q, cot, qgain, keys, vals, mask)
        for h in range(8):
            out_q[0:64, col(8 * c, h)] = dq[h * 64:(h + 1) * 64].astype(BF)
        dkp[:, col(c, 0)] = dk[:64]
        dvp[:, col(c, 0)] = dv[:64]
        x = pre_k[:, col(c, 0)].astype(F32)
        k_term = jnp.sum(dk[:64] * x * inverse_norm(x), axis=0, keepdims=True)
        k_term += jnp.sum(dk[64:] * far_k.astype(F32), axis=0, keepdims=True) / kgain
        g[0:1] += q_term
        g[1:2] += k_term
        for b in range(4):
            t0[8 * b + c] = dk[64 + 16 * b:80 + 16 * b].astype(BF)
            t0[8 * b + 4 + c] = dv[64 + 16 * b:80 + 16 * b].astype(BF)

    peers(lambda t: copy(4, t0.at[t], rt0.at[me], t).start())
    rt0[me] = t0[me]

    back = (8 * ((iota((64, 64), 1) % 16) // 2) + 2 * (iota((64, 64), 1) // 16) + iota((64, 64), 1) % 2
            == iota((64, 64), 0)).astype(F32).astype(BF)
    upper_ok = (my_upper >= 0).astype(F32)

    @pl.loop(0, 4)
    def _(step):
        c = (me // 8 + 4 - step) % 4

        @pl.loop(0, 8)
        def _(h):
            @pl.when(8 * c + h != me)
            def _():
                await_recv(3, r2b.at[pl.ds((8 * c + h) * 8, 8)], 8 * c + h)

        col = lambda base, h: pl.ds(pl.multiple_of((base + h) * 128, 128), 128)
        both = r2b[pl.ds(64 * c, 64)].astype(F32)
        q = both[:, :8].reshape(512, 128)
        cot = (both[:, 8:].reshape(512, 128) * adv).astype(BF)
        x = contract(back, tiles(r2a, 3, c), 1, 0)
        r = inverse_norm(x)
        far_k = jnp.concatenate([tiles(r2a, 1, c), tiles(r2a, 2, c)], axis=0)
        keys = jnp.concatenate([(x * r * kgain).astype(BF), far_k], axis=0)
        vals = jnp.concatenate(
            [contract(back, tiles(r2a, 3, 4 + c), 1, 0).astype(BF), tiles(r2a, 1, 4 + c), tiles(r2a, 2, 4 + c)], axis=0
        )
        ones = jnp.full((64, 512), 1.0, F32)
        mask = jnp.concatenate([causal[...], ones, ones * upper_ok], axis=0)
        dq, dk, dv, q_term = attend(q, cot, qgain, keys, vals, mask)
        for h in range(8):
            out_q[64:128, col(8 * c, h)] = dq[h * 64:(h + 1) * 64].astype(BF)
        out_k[64:128, col(c, 0)] = norm_back(x, r, kgain, dk[:64]).astype(BF)
        out_v[64:128, col(c, 0)] = dv[:64].astype(BF)
        k_term = jnp.sum(dk[:64] * x * r, axis=0, keepdims=True)
        k_term += jnp.sum(dk[64:] * far_k.astype(F32), axis=0, keepdims=True) / kgain
        g[0:1] += q_term
        g[1:2] += k_term
        for b in range(4):
            for j in range(2):
                at = 64 + 64 * j + 16 * b
                t12[8 * b + c, j] = dk[at:at + 16].astype(BF)
                t12[8 * b + 4 + c, j] = dv[at:at + 16].astype(BF)

    peers(lambda t: copy(5, t12.at[t], rt12.at[me], t).start())
    rt12[me] = t12[me]
    peers(lambda t: copy(6, g, rg.at[me], t).start())
    rg[me] = g[...]

    peers(lambda t: await_recv(4, rt0.at[t], t))
    total = contract(m0[...], rt0[...].reshape(512, 128), 1, 0)
    peers(lambda t: await_recv(5, rt12.at[t], t))
    total += contract(m12[...], rt12[...].reshape(1024, 128), 1, 0)
    s4[...] = total.astype(BF).reshape(N, 16, 128)
    peers(lambda t: copy(7, s4.at[t], r4.at[me], t).start())
    r4[me] = s4[me]

    peers(lambda t: await_recv(6, rg.at[t], t))
    gd[...] = jnp.sum(rg[...], axis=0)

    def dp_copy(k):
        t = dp_peer(k)
        return pltpu.make_async_remote_copy(
            src_ref=gd, dst_ref=rd.at[group], send_sem=dsend.at[t], recv_sem=drecv.at[group],
            device_id={"dp": t}, device_id_type=MESH,
        )

    @pl.loop(1, n_dp)
    def _(k):
        dp_copy(k).start()

    rd[group] = gd[...]

    peers(lambda t: await_recv(7, r4.at[t], t))
    for c in range(4):
        cols = slice(c * 128, (c + 1) * 128)
        x = pre_k[:, cols].astype(F32)
        dk = dkp[:, cols] + tiles(r4, None, c).astype(F32)
        out_k[0:64, cols] = norm_back(x, inverse_norm(x), kgain, dk).astype(BF)
        out_v[0:64, cols] = (dvp[:, cols] + tiles(r4, None, 4 + c).astype(F32)).astype(BF)

    @pl.loop(1, n_dp)
    def _(k):
        t = dp_peer(k)
        pltpu.make_async_copy(rd.at[t], rd.at[t], drecv.at[t]).wait()

    sums = jnp.sum(rd[...], axis=0)
    out_qg[...] = sums[0:1]
    out_kg[...] = sums[1:2]

    def drain(t):
        await_send(0, fragment(t), t)
        await_send(1, s1b.at[pl.ds(t * 8, 8)], t)
        await_send(2, s2a.at[t], t)
        await_send(3, s2b.at[pl.ds(t * 8, 8)], t)
        await_send(4, t0.at[t], t)
        await_send(5, t12.at[t], t)
        await_send(6, g, t)
        await_send(7, s4.at[t], t)

    peers(drain)

    @pl.loop(1, n_dp)
    def _(k):
        t = dp_peer(k)
        pltpu.make_async_copy(gd, gd, dsend.at[t]).wait()


def body(
    pre_q, prefix_keys, prefix_values, pre_cot, gen_q, rollout_keys, rollout_values, gen_cot,
    q_gain, k_gain, piece_dest, prefix_parent, branch_parent, rewards,
):
    n_dp = lax.axis_size("dp")
    piece = jnp.arange(256, dtype=jnp.int32)
    inverse = jnp.sum(
        jnp.where(piece_dest[0][:, None] == piece[None, :], piece[:, None], 0), axis=0, dtype=jnp.int32
    )[None]
    vmem = pl.BlockSpec(memory_space=pltpu.VMEM)
    smem = pl.BlockSpec(memory_space=pltpu.SMEM)
    out_q, out_k, out_v, out_qg, out_kg = pl.pallas_call(
        kernel,
        out_shape=(
            jax.ShapeDtypeStruct((128, 4096), BF),
            jax.ShapeDtypeStruct((128, 512), BF),
            jax.ShapeDtypeStruct((128, 512), BF),
            jax.ShapeDtypeStruct((1, 128), F32),
            jax.ShapeDtypeStruct((1, 128), F32),
        ),
        in_specs=[vmem] * 14 + [smem] * 4,
        out_specs=[vmem] * 5,
        scratch_shapes=[
            pltpu.VMEM((2, 64, 1024), BF),
            pltpu.VMEM((N, 2, 16, 128), BF),
            pltpu.VMEM((256, 16, 128), BF),
            pltpu.VMEM((256, 16, 128), BF),
            pltpu.VMEM((N, 4, 16, 128), BF),
            pltpu.VMEM((N, 4, 16, 128), BF),
            pltpu.VMEM((256, 16, 128), BF),
            pltpu.VMEM((256, 16, 128), BF),
            pltpu.VMEM((N, 16, 128), BF),
            pltpu.VMEM((N, 16, 128), BF),
            pltpu.VMEM((N, 2, 16, 128), BF),
            pltpu.VMEM((N, 2, 16, 128), BF),
            pltpu.VMEM((N, 16, 128), BF),
            pltpu.VMEM((N, 16, 128), BF),
            pltpu.VMEM((8, 128), F32),
            pltpu.VMEM((N, 8, 128), F32),
            pltpu.VMEM((8, 128), F32),
            pltpu.VMEM((n_dp, 8, 128), F32),
            pltpu.VMEM((512, 512), BF),
            pltpu.VMEM((512, 1024), BF),
            pltpu.VMEM((64, 512), F32),
            pltpu.VMEM((64, 512), F32),
            pltpu.VMEM((64, 512), F32),
            pltpu.SemaphoreType.DMA((8, N)),
            pltpu.SemaphoreType.DMA((8, N)),
            pltpu.SemaphoreType.DMA((n_dp,)),
            pltpu.SemaphoreType.DMA((n_dp,)),
        ],
        compiler_params=pltpu.CompilerParams(
            collective_id=0, has_side_effects=True, vmem_limit_bytes=40 * 1024 * 1024
        ),
    )(
        pre_q, prefix_keys, prefix_values, pre_cot, gen_q, rollout_keys, rollout_values, gen_cot,
        q_gain.reshape(1, 128), k_gain.reshape(1, 128),
        piece_dest, prefix_parent, branch_parent, rewards,
        inverse, prefix_parent, branch_parent, rewards,
    )
    return out_q, out_k, out_v, out_qg.reshape(128), out_kg.reshape(128)


def solution(mesh):
    rows = P(("dp", "ctx"), None)
    return jax.shard_map(
        body,
        mesh=mesh,
        in_specs=(rows,) * 8 + (P(), P()) + (P("dp", None),) * 4,
        out_specs=(rows, rows, rows, P(), P()),
        check_vma=False,
    )
```

```python
import math

import jax
import jax.numpy as jnp
from jax import lax
from jax.experimental import pallas as pl
from jax.experimental.pallas import tpu as pltpu
from jax.sharding import PartitionSpec as P

EPSILON = 1e-06
NZ, NY = 8, 4
N = NZ * NY
BF = jnp.bfloat16
F32 = jnp.float32
MESH = pl.DeviceIdType.MESH
SCALE = 1.0 / math.sqrt(128)


def iota(shape, axis):
    return lax.broadcasted_iota(jnp.int32, shape, axis)


def contract(a, b, da, db):
    return lax.dot_general(a, b, (((da,), (db,)), ((), ())), preferred_element_type=F32)


def inverse_norm(x):
    return lax.rsqrt(jnp.mean(x * x, axis=-1, keepdims=True) + EPSILON)


def norm_back(x, r, gain, upstream):
    scaled = gain * upstream
    inner = jnp.mean(x * scaled, axis=-1, keepdims=True)
    return r * scaled - x * (r * r * r) * inner


def attend(q, cot, gain, keys, vals, mask):
    r = inverse_norm(q)
    qn = (q * r * gain).astype(BF)
    weights = jnp.exp(contract(keys, qn, 1, 1) * SCALE) * mask
    probs = weights * (1.0 / jnp.sum(weights, axis=0, keepdims=True))
    dprob = contract(vals, cot, 1, 1)
    inner = jnp.sum(probs * dprob, axis=0, keepdims=True)
    dscore = (probs * (dprob - inner) * SCALE).astype(BF)
    dq = contract(dscore, keys, 0, 0)
    dk = contract(dscore, qn, 1, 0)
    dv = contract(probs.astype(BF), cot, 1, 0)
    gain_term = jnp.sum(dq * q * r, axis=0, keepdims=True)
    return norm_back(q, r, gain, dq), dk, dv, gain_term


def kernel(*refs):
    ins, outs, rest = refs[:14], refs[14:19], refs[19:]
    held, small, (table, loaded, indexed) = rest[:14], rest[14:18], rest[18:21]
    compute(ins, outs, rest[21:26], held, small, table, loaded, indexed, *rest[26:])


def compute(
    ins, outs, staged, held, small, table, loaded, indexed,
    stored, kv, r1a, s1b, r1b, s2a, r2a, s2b, r2b, t0, rt0, t12, rt12, s4, r4,
    g, rg, gd, rd, m0, m12, dkp, dvp, causal, send, recv, dsend, drecv,
):
    pre_q, pre_k, pre_v, pre_c, gen_q, gen_k, gen_v, gen_c, qg, kg, dest_row, pp_row, bp_row, rew_row = held
    inv_s, pp_s, bp_s, rew_s = small
    out_q, out_k, out_v, out_qg, out_kg = staged
    me = lax.axis_index("ctx")
    group = lax.axis_index("dp")
    n_dp = lax.axis_size("dp")

    def peer(k):
        j = k // NY
        dz = jnp.where(j % 2 == 1, (j + 1) // 2, (NZ - j // 2) % NZ)
        return ((me // NY + dz) % NZ) * NY + (me % NY + k % NY) % NY

    def dp_peer(k):
        return (group + k) % n_dp

    def copy(stage, src, dst, target):
        return pltpu.make_async_remote_copy(
            src_ref=src, dst_ref=dst, send_sem=send.at[stage, target], recv_sem=recv.at[stage, me],
            device_id={"ctx": target}, device_id_type=MESH,
        )

    def await_recv(stage, dst, source):
        pltpu.make_async_copy(dst, dst, recv.at[stage, source]).wait()

    def await_send(stage, src, target):
        pltpu.make_async_copy(src, src, send.at[stage, target]).wait()

    def peers(body):
        @pl.loop(1, N)
        def _(k):
            body(peer(k))

    def store(i, output, rows):
        return pltpu.make_async_copy(staged[output].at[rows], outs[output].at[rows], stored.at[i])

    upper_half, lower_half = pl.ds(0, 64), pl.ds(64, 64)
    stores = [
        store(0, 0, upper_half), store(1, 1, lower_half), store(2, 2, lower_half),
        store(3, 1, upper_half), store(4, 2, upper_half), store(5, 3, pl.ds(0, 1)), store(6, 4, pl.ds(0, 1)),
    ]

    def store_branch(c):
        at = (lower_half, pl.ds(pl.multiple_of(1024 * c, 128), 1024))
        return pltpu.make_async_copy(staged[0].at[at], outs[0].at[at], stored.at[7 + c])

    barrier = pltpu.get_barrier_semaphore()

    @pl.loop(1, N)
    def _(k):
        pl.semaphore_signal(barrier, inc=1, device_id={"ctx": peer(k)}, device_id_type=MESH)

    @pl.loop(1, n_dp)
    def _(k):
        pl.semaphore_signal(barrier, inc=1, device_id={"dp": dp_peer(k)}, device_id_type=MESH)

    fetch = [pltpu.make_async_copy(ins[i], held[i], loaded.at[i]) for i in range(14)]
    fetch += [pltpu.make_async_copy(ins[i], small[i - 10], indexed.at[i - 10]) for i in (11, 12, 13)]
    for i in (8, 9, 1, 2, 5, 6, 4, 7, 10, 11, 12, 13, 14, 15, 16, 0, 3):
        fetch[i].start()
    for i in (8, 9, 1, 2, 5, 6):
        fetch[i].wait()

    kgain = kg[...]
    qgain = qg[...]

    for c in range(4):
        x = pre_k[:, c * 128:(c + 1) * 128].astype(F32)
        kv[0, :, c * 128:(c + 1) * 128] = (x * inverse_norm(x) * kgain).astype(BF)
    kv[0, :, 512:] = pre_v[...]
    rows = iota((64, 64), 0)
    spread = (8 * ((rows % 16) // 2) + 2 * (rows // 16) + rows % 2 == iota((64, 64), 1)).astype(F32).astype(BF)
    kv[1, :, :512] = contract(spread, gen_k[...], 1, 0).astype(BF)
    kv[1, :, 512:] = contract(spread, gen_v[...], 1, 0).astype(BF)

    for i in (4, 7):
        fetch[i].wait()
    pl.semaphore_wait(barrier, N - 1 + n_dp - 1)

    def fragment(t):
        rb = pl.multiple_of((t // 8) * 16, 16)
        cb = pl.multiple_of((t % 8) * 128, 128)
        return kv.at[:, pl.ds(rb, 16), pl.ds(cb, 128)]

    def send_1a(t):
        copy(0, fragment(t), r1a.at[me], t).start()

    peers(send_1a)
    r1a[me] = fragment(me)[...]

    def slab(t):
        cols = pl.ds(pl.multiple_of(t * 128, 128), 128)
        q = gen_q[:, cols].astype(F32).reshape(8, 8, 128)
        c = gen_c[:, cols].astype(F32).reshape(8, 8, 128)
        return jnp.concatenate([q, c], axis=1).astype(BF)

    def send_1b(t):
        part = s1b.at[pl.ds(t * 8, 8)]
        part[...] = slab(t)
        copy(1, part, r1b.at[pl.ds(me * 8, 8)], t).start()

    peers(send_1b)
    r1b[pl.ds(me * 8, 8)] = slab(me)

    for i in (10, 11, 12, 13, 14, 15, 16):
        fetch[i].wait()
    column = jnp.broadcast_to(dest_row[...], (128, 256)).T
    for half in range(2):
        hit = column == iota((256, 128), 1) + 128 * half
        table[:, half * 128:(half + 1) * 128] = jnp.max(jnp.where(hit, iota((256, 128), 0), 0), axis=0, keepdims=True)
    lookup = pltpu.make_async_copy(table, inv_s, indexed.at[0])
    lookup.start()
    pp = jnp.broadcast_to(pp_row[...].astype(F32), (8, N))
    bp = jnp.broadcast_to(bp_row[...].astype(F32), (8, N))
    pick = (bp_row[...] == iota((N, N), 0)).astype(F32).astype(BF)
    upper = contract(pp.astype(BF), pick, 1, 0)
    spread0 = (iota((N, 512), 0) == iota((N, 512), 1) // 16).astype(F32).astype(BF)
    row0 = (iota((8, 512), 1) % 16).astype(F32)
    spread1 = (iota((N, 1024), 0) == iota((N, 1024), 1) // 32).astype(F32).astype(BF)
    lane1 = iota((8, 1024), 1)
    id0 = contract(pp.astype(BF), spread0, 1, 0) * 16.0 + row0
    parent1 = contract(bp.astype(BF), spread1, 1, 0)
    upper1 = contract(upper.astype(BF), spread1, 1, 0)
    id1 = jnp.where((lane1 // 16) % 2 == 0, parent1, upper1) * 16.0 + (lane1 % 16).astype(F32)
    m0[...] = (iota((512, 512), 0).astype(F32) == id0[:1]).astype(F32).astype(BF)
    m12[...] = (iota((512, 1024), 0).astype(F32) == id1[:1]).astype(F32).astype(BF)
    dest = jnp.broadcast_to(dest_row[...].astype(F32), (8, 256)).astype(BF)
    spread2 = (iota((256, 512), 0) == iota((256, 512), 1) // 2).astype(F32).astype(BF)
    id2 = contract(dest, spread2, 1, 0) * 2.0 + (iota((8, 512), 1) % 2).astype(F32)
    order = (iota((512, 512), 0).astype(F32) == id2[:1]).astype(F32).astype(BF)
    causal[...] = (iota((64, 512), 0) <= iota((64, 512), 1) % 64).astype(F32)

    my_parent = bp_s[0, me]
    my_upper = pp_s[0, my_parent]
    my_above = pp_s[0, me]
    my_root = jnp.where(my_upper >= 0, my_upper, my_parent).astype(F32)
    root = jnp.where(upper >= 0.0, upper, bp)
    member = (root == my_root).astype(F32)
    score = jnp.broadcast_to(rew_row[...].astype(F32), (8, N))
    size = jnp.sum(member, axis=1, keepdims=True)
    center = jnp.sum(member * score, axis=1, keepdims=True) / size
    var = jnp.sum(member * (score - center) ** 2, axis=1, keepdims=True) / size
    adv = ((rew_s[0, me].astype(F32) - center) / jnp.maximum(jnp.sqrt(var), 1.0))[:1]

    peers(lambda t: await_recv(0, r1a.at[t], t))
    s2a[:, 3] = contract(order, r1a[:, 1].reshape(512, 128), 1, 0).astype(BF).reshape(N, 16, 128)

    def fill_2a(t):
        parent = bp_s[0, t]
        s2a[t, 0] = r1a[jnp.maximum(pp_s[0, t], 0), 0]
        s2a[t, 1] = r1a[parent, 0]
        s2a[t, 2] = r1a[jnp.maximum(pp_s[0, parent], 0), 0]

    def send_2a(t):
        fill_2a(t)
        copy(2, s2a.at[t], r2a.at[me], t).start()

    peers(send_2a)
    fill_2a(me)
    r2a[me] = s2a[me]

    lookup.wait()
    peers(lambda t: await_recv(1, r1b.at[pl.ds(t * 8, 8)], t))

    def send_2b(t):
        for p in range(8):
            s2b[t * 8 + p] = r1b[inv_s[0, t * 8 + p]]
        copy(3, s2b.at[pl.ds(t * 8, 8)], r2b.at[pl.ds(me * 8, 8)], t).start()

    peers(send_2b)
    for p in range(8):
        r2b[me * 8 + p] = r1b[inv_s[0, me * 8 + p]]

    def tiles(ref, at, c):
        return jnp.concatenate([ref[8 * b + c] if at is None else ref[8 * b + c, at] for b in range(4)], axis=0)

    for i in (0, 3):
        fetch[i].wait()
    peers(lambda t: await_recv(2, r2a.at[t], t))
    g[...] = jnp.zeros((8, 128), F32)
    above = (my_above >= 0).astype(F32)

    @pl.loop(0, 4)
    def _(c):
        col = lambda base, h: pl.ds(pl.multiple_of((base + h) * 128, 128), 128)
        q = jnp.concatenate([pre_q[:, col(8 * c, h)] for h in range(8)], axis=0).astype(F32)
        cot = jnp.concatenate([pre_c[:, col(8 * c, h)] for h in range(8)], axis=0)
        own_k = kv[0, :, col(c, 0)]
        far_k = tiles(r2a, 0, c)
        keys = jnp.concatenate([own_k, far_k], axis=0)
        vals = jnp.concatenate([kv[0, :, col(c, 4)], tiles(r2a, 0, 4 + c)], axis=0)
        mask = jnp.concatenate([causal[...], jnp.full((64, 512), 1.0, F32) * above], axis=0)
        dq, dk, dv, q_term = attend(q, cot, qgain, keys, vals, mask)
        for h in range(8):
            out_q[0:64, col(8 * c, h)] = dq[h * 64:(h + 1) * 64].astype(BF)
        dkp[:, col(c, 0)] = dk[:64]
        dvp[:, col(c, 0)] = dv[:64]
        x = pre_k[:, col(c, 0)].astype(F32)
        k_term = jnp.sum(dk[:64] * x * inverse_norm(x), axis=0, keepdims=True)
        k_term += jnp.sum(dk[64:] * far_k.astype(F32), axis=0, keepdims=True) / kgain
        g[0:1] += q_term
        g[1:2] += k_term
        for b in range(4):
            t0[8 * b + c] = dk[64 + 16 * b:80 + 16 * b].astype(BF)
            t0[8 * b + 4 + c] = dv[64 + 16 * b:80 + 16 * b].astype(BF)

    stores[0].start()
    peers(lambda t: copy(4, t0.at[t], rt0.at[me], t).start())
    rt0[me] = t0[me]

    def drain_early(t):
        await_send(0, fragment(t), t)
        await_send(1, s1b.at[pl.ds(t * 8, 8)], t)
        await_send(2, s2a.at[t], t)

    peers(drain_early)

    back = (8 * ((iota((64, 64), 1) % 16) // 2) + 2 * (iota((64, 64), 1) // 16) + iota((64, 64), 1) % 2
            == iota((64, 64), 0)).astype(F32).astype(BF)
    upper_ok = (my_upper >= 0).astype(F32)

    @pl.loop(0, 4)
    def _(step):
        c = (me // 8 + jnp.where(step < 2, step, 5 - step)) % 4

        @pl.loop(0, 8)
        def _(h):
            @pl.when(8 * c + h != me)
            def _():
                await_recv(3, r2b.at[pl.ds((8 * c + h) * 8, 8)], 8 * c + h)

        col = lambda base, h: pl.ds(pl.multiple_of((base + h) * 128, 128), 128)
        both = r2b[pl.ds(64 * c, 64)].astype(F32)
        q = both[:, :8].reshape(512, 128)
        cot = (both[:, 8:].reshape(512, 128) * adv).astype(BF)
        x = contract(back, tiles(r2a, 3, c), 1, 0)
        r = inverse_norm(x)
        far_k = jnp.concatenate([tiles(r2a, 1, c), tiles(r2a, 2, c)], axis=0)
        keys = jnp.concatenate([(x * r * kgain).astype(BF), far_k], axis=0)
        vals = jnp.concatenate(
            [contract(back, tiles(r2a, 3, 4 + c), 1, 0).astype(BF), tiles(r2a, 1, 4 + c), tiles(r2a, 2, 4 + c)], axis=0
        )
        ones = jnp.full((64, 512), 1.0, F32)
        mask = jnp.concatenate([causal[...], ones, ones * upper_ok], axis=0)
        dq, dk, dv, q_term = attend(q, cot, qgain, keys, vals, mask)
        for h in range(8):
            out_q[64:128, col(8 * c, h)] = dq[h * 64:(h + 1) * 64].astype(BF)
        out_k[64:128, col(c, 0)] = norm_back(x, r, kgain, dk[:64]).astype(BF)
        out_v[64:128, col(c, 0)] = dv[:64].astype(BF)
        k_term = jnp.sum(dk[:64] * x * r, axis=0, keepdims=True)
        k_term += jnp.sum(dk[64:] * far_k.astype(F32), axis=0, keepdims=True) / kgain
        g[0:1] += q_term
        g[1:2] += k_term
        for b in range(4):
            for j in range(2):
                at = 64 + 64 * j + 16 * b
                t12[8 * b + c, j] = dk[at:at + 16].astype(BF)
                t12[8 * b + 4 + c, j] = dv[at:at + 16].astype(BF)
        store_branch(c).start()
        for b in range(8):
            t = 4 * b + c

            @pl.when(t != me)
            def _():
                copy(5, t12.at[t], rt12.at[me], t).start()

    rt12[me] = t12[me]
    stores[1].start()
    stores[2].start()
    peers(lambda t: copy(6, g, rg.at[me], t).start())
    rg[me] = g[...]

    peers(lambda t: await_recv(4, rt0.at[t], t))
    total = contract(m0[...], rt0[...].reshape(512, 128), 1, 0)

    def drain_later(t):
        await_send(3, s2b.at[pl.ds(t * 8, 8)], t)
        await_send(4, t0.at[t], t)

    peers(drain_later)
    peers(lambda t: await_recv(5, rt12.at[t], t))
    total += contract(m12[...], rt12[...].reshape(1024, 128), 1, 0)
    s4[...] = total.astype(BF).reshape(N, 16, 128)
    peers(lambda t: copy(7, s4.at[t], r4.at[me], t).start())
    r4[me] = s4[me]

    peers(lambda t: await_recv(6, rg.at[t], t))
    gd[...] = jnp.sum(rg[...], axis=0)

    def dp_copy(k):
        t = dp_peer(k)
        return pltpu.make_async_remote_copy(
            src_ref=gd, dst_ref=rd.at[group], send_sem=dsend.at[t], recv_sem=drecv.at[group],
            device_id={"dp": t}, device_id_type=MESH,
        )

    @pl.loop(1, n_dp)
    def _(k):
        dp_copy(k).start()

    rd[group] = gd[...]

    peers(lambda t: await_recv(7, r4.at[t], t))
    for c in range(4):
        cols = slice(c * 128, (c + 1) * 128)
        x = pre_k[:, cols].astype(F32)
        dk = dkp[:, cols] + tiles(r4, None, c).astype(F32)
        out_k[0:64, cols] = norm_back(x, inverse_norm(x), kgain, dk).astype(BF)
        out_v[0:64, cols] = (dvp[:, cols] + tiles(r4, None, 4 + c).astype(F32)).astype(BF)

    stores[3].start()
    stores[4].start()

    @pl.loop(1, n_dp)
    def _(k):
        t = dp_peer(k)
        pltpu.make_async_copy(rd.at[t], rd.at[t], drecv.at[t]).wait()

    sums = jnp.sum(rd[...], axis=0)
    out_qg[...] = sums[0:1]
    out_kg[...] = sums[1:2]
    stores[5].start()
    stores[6].start()

    def drain(t):
        await_send(5, t12.at[t], t)
        await_send(6, g, t)
        await_send(7, s4.at[t], t)

    peers(drain)

    @pl.loop(1, n_dp)
    def _(k):
        t = dp_peer(k)
        pltpu.make_async_copy(gd, gd, dsend.at[t]).wait()

    for each in stores:
        each.wait()

    @pl.loop(0, 4)
    def _(c):
        store_branch(c).wait()


def write_out(*refs):
    src, dst, mid = refs[:5], refs[5:10], refs[10:15]
    loads, stores = refs[15:]
    chunks = [(0, pl.ds(32 * i, 32)) for i in range(4)] + [(1, pl.ds(0, 128)), (2, pl.ds(0, 128))]
    chunks += [(3, pl.ds(0, 1)), (4, pl.ds(0, 1))]
    load = [pltpu.make_async_copy(src[a].at[r], mid[a].at[r], loads.at[n]) for n, (a, r) in enumerate(chunks)]
    store = [pltpu.make_async_copy(mid[a].at[r], dst[a].at[r], stores.at[n]) for n, (a, r) in enumerate(chunks)]
    for each in load:
        each.start()
    for first, then in zip(load, store):
        first.wait()
        then.start()
    for each in store:
        each.wait()


def body(
    pre_q, prefix_keys, prefix_values, pre_cot, gen_q, rollout_keys, rollout_values, gen_cot,
    q_gain, k_gain, piece_dest, prefix_parent, branch_parent, rewards,
):
    n_dp = lax.axis_size("dp")
    hbm = pl.BlockSpec(memory_space=pl.ANY)
    out_q, out_k, out_v, out_qg, out_kg = pl.pallas_call(
        kernel,
        out_shape=(
            jax.ShapeDtypeStruct((128, 4096), BF),
            jax.ShapeDtypeStruct((128, 512), BF),
            jax.ShapeDtypeStruct((128, 512), BF),
            jax.ShapeDtypeStruct((1, 128), F32),
            jax.ShapeDtypeStruct((1, 128), F32),
        ),
        in_specs=[hbm] * 14,
        out_specs=[hbm] * 5,
        scratch_shapes=[
            pltpu.VMEM((64, 4096), BF),
            pltpu.VMEM((64, 512), BF),
            pltpu.VMEM((64, 512), BF),
            pltpu.VMEM((64, 4096), BF),
            pltpu.VMEM((64, 4096), BF),
            pltpu.VMEM((64, 512), BF),
            pltpu.VMEM((64, 512), BF),
            pltpu.VMEM((64, 4096), BF),
            pltpu.VMEM((1, 128), F32),
            pltpu.VMEM((1, 128), F32),
            pltpu.VMEM((1, 256), jnp.int32),
            pltpu.VMEM((1, N), jnp.int32),
            pltpu.VMEM((1, N), jnp.int32),
            pltpu.VMEM((1, N), jnp.int32),
            pltpu.SMEM((1, 256), jnp.int32),
            pltpu.SMEM((1, N), jnp.int32),
            pltpu.SMEM((1, N), jnp.int32),
            pltpu.SMEM((1, N), jnp.int32),
            pltpu.VMEM((1, 256), jnp.int32),
            pltpu.SemaphoreType.DMA((14,)),
            pltpu.SemaphoreType.DMA((4,)),
            pltpu.VMEM((128, 4096), BF),
            pltpu.VMEM((128, 512), BF),
            pltpu.VMEM((128, 512), BF),
            pltpu.VMEM((1, 128), F32),
            pltpu.VMEM((1, 128), F32),
            pltpu.SemaphoreType.DMA((11,)),
            pltpu.VMEM((2, 64, 1024), BF),
            pltpu.VMEM((N, 2, 16, 128), BF),
            pltpu.VMEM((256, 16, 128), BF),
            pltpu.VMEM((256, 16, 128), BF),
            pltpu.VMEM((N, 4, 16, 128), BF),
            pltpu.VMEM((N, 4, 16, 128), BF),
            pltpu.VMEM((256, 16, 128), BF),
            pltpu.VMEM((256, 16, 128), BF),
            pltpu.VMEM((N, 16, 128), BF),
            pltpu.VMEM((N, 16, 128), BF),
            pltpu.VMEM((N, 2, 16, 128), BF),
            pltpu.VMEM((N, 2, 16, 128), BF),
            pltpu.VMEM((N, 16, 128), BF),
            pltpu.VMEM((N, 16, 128), BF),
            pltpu.VMEM((8, 128), F32),
            pltpu.VMEM((N, 8, 128), F32),
            pltpu.VMEM((8, 128), F32),
            pltpu.VMEM((n_dp, 8, 128), F32),
            pltpu.VMEM((512, 512), BF),
            pltpu.VMEM((512, 1024), BF),
            pltpu.VMEM((64, 512), F32),
            pltpu.VMEM((64, 512), F32),
            pltpu.VMEM((64, 512), F32),
            pltpu.SemaphoreType.DMA((8, N)),
            pltpu.SemaphoreType.DMA((8, N)),
            pltpu.SemaphoreType.DMA((n_dp,)),
            pltpu.SemaphoreType.DMA((n_dp,)),
        ],
        compiler_params=pltpu.CompilerParams(
            collective_id=0, has_side_effects=True, vmem_limit_bytes=60 * 1024 * 1024
        ),
    )(
        pre_q, prefix_keys, prefix_values, pre_cot, gen_q, rollout_keys, rollout_values, gen_cot,
        q_gain.reshape(1, 128), k_gain.reshape(1, 128),
        piece_dest, prefix_parent, branch_parent, rewards,
    )
    results = (out_q, out_k, out_v, out_qg, out_kg)
    out_q, out_k, out_v, out_qg, out_kg = pl.pallas_call(
        write_out,
        out_shape=tuple(jax.ShapeDtypeStruct(x.shape, x.dtype) for x in results),
        in_specs=[hbm] * 5,
        out_specs=[hbm] * 5,
        scratch_shapes=[pltpu.VMEM(x.shape, x.dtype) for x in results]
        + [pltpu.SemaphoreType.DMA((8,)), pltpu.SemaphoreType.DMA((8,))],
    )(*results)
    return out_q, out_k, out_v, out_qg.reshape(128), out_kg.reshape(128)


def solution(mesh):
    rows = P(("dp", "ctx"), None)
    return jax.shard_map(
        body,
        mesh=mesh,
        in_specs=(rows,) * 8 + (P(), P()) + (P("dp", None),) * 4,
        out_specs=(rows, rows, rows, P(), P()),
        check_vma=False,
    )
```

```python
import math

import jax
import jax.numpy as jnp
from jax import lax
from jax.experimental import pallas as pl
from jax.experimental.pallas import tpu as pltpu
from jax.sharding import PartitionSpec as P

EPSILON = 1e-06
NZ, NY = 8, 4
N = NZ * NY
BF = jnp.bfloat16
F32 = jnp.float32
MESH = pl.DeviceIdType.MESH
SCALE = 1.0 / math.sqrt(128)


def iota(shape, axis):
    return lax.broadcasted_iota(jnp.int32, shape, axis)


def contract(a, b, da, db):
    return lax.dot_general(a, b, (((da,), (db,)), ((), ())), preferred_element_type=F32)


def inverse_norm(x):
    return lax.rsqrt(jnp.mean(x * x, axis=-1, keepdims=True) + EPSILON)


def norm_back(x, r, gain, upstream):
    scaled = gain * upstream
    inner = jnp.mean(x * scaled, axis=-1, keepdims=True)
    return r * scaled - x * (r * r * r) * inner


def attend(q, cot, gain, keys, vals, mask):
    r = inverse_norm(q)
    qn = (q * r * gain).astype(BF)
    weights = jnp.exp(contract(keys, qn, 1, 1) * SCALE) * mask
    probs = weights * (1.0 / jnp.sum(weights, axis=0, keepdims=True))
    dprob = contract(vals, cot, 1, 1)
    inner = jnp.sum(probs * dprob, axis=0, keepdims=True)
    dscore = (probs * (dprob - inner) * SCALE).astype(BF)
    dq = contract(dscore, keys, 0, 0)
    dk = contract(dscore, qn, 1, 0)
    dv = contract(probs.astype(BF), cot, 1, 0)
    gain_term = jnp.sum(dq * q * r, axis=0, keepdims=True)
    return norm_back(q, r, gain, dq), dk, dv, gain_term


def kernel(*refs):
    ins, outs, rest = refs[:14], refs[14:19], refs[19:]
    held, small, (table, loaded, indexed) = rest[:14], rest[14:18], rest[18:21]
    compute(ins, outs, rest[21:26], held, small, table, loaded, indexed, *rest[26:])


def compute(
    ins, outs, staged, held, small, table, loaded, indexed,
    stored, kv, r1a, s1b, r1b, s2a, r2a, s2b, r2b, t0, rt0, t12, rt12, s4, r4,
    g, rg, gd, rd, m0, m12, dkp, dvp, causal, send, recv, dsem,
):
    pre_q, pre_k, pre_v, pre_c, gen_q, gen_k, gen_v, gen_c, qg, kg, dest_row, pp_row, bp_row, rew_row = held
    inv_s, pp_s, bp_s, rew_s = small
    out_q, out_k, out_v, out_qg, out_kg = staged
    me = lax.axis_index("ctx")
    group = lax.axis_index("dp")
    n_dp = lax.axis_size("dp")

    def peer(k):
        j, m = lax.div(k, NY), lax.rem(k, NY)
        dz = NZ + NZ // 2 + lax.div(j + 1, 2) * (1 - 2 * lax.rem(j, 2))
        dy = NY + NY // 2 + lax.div(m + 1, 2) * (1 - 2 * lax.rem(m, 2))
        return lax.rem(lax.div(me, NY) + dz, NZ) * NY + lax.rem(me + dy, NY)

    def dp_peer(k):
        return lax.rem(group + k, n_dp)

    def copy(stage, src, dst, target):
        arrived = recv.at[8 + lax.div(me, 8)] if stage == 3 else recv.at[stage]
        return pltpu.make_async_remote_copy(
            src_ref=src, dst_ref=dst, send_sem=send.at[stage], recv_sem=arrived,
            device_id={"ctx": target}, device_id_type=MESH,
        )

    def await_all(sem, ref):
        pltpu.make_async_copy(ref, ref, sem).wait()

    def peers(body):
        @pl.loop(0, N - 1)
        def _(k):
            body(peer(k))

    def others(ref, size=1):
        return ref.at[pl.ds(0, (N - 1) * size)]

    def store(i, output, rows):
        return pltpu.make_async_copy(staged[output].at[rows], outs[output].at[rows], stored.at[i])

    upper_half, lower_half = pl.ds(0, 64), pl.ds(64, 64)
    stores = [
        store(0, 0, upper_half), store(1, 1, lower_half), store(2, 2, lower_half),
        store(3, 1, upper_half), store(4, 2, upper_half), store(5, 3, pl.ds(0, 1)), store(6, 4, pl.ds(0, 1)),
    ]

    def store_branch(c):
        at = (lower_half, pl.ds(pl.multiple_of(1024 * c, 128), 1024))
        return pltpu.make_async_copy(staged[0].at[at], outs[0].at[at], stored.at[7 + c])

    barrier = pltpu.get_barrier_semaphore()

    def greet(t):
        pl.semaphore_signal(barrier, inc=1, device_id={"ctx": t}, device_id_type=MESH)

    peers(greet)

    @pl.loop(1, n_dp)
    def _(k):
        pl.semaphore_signal(barrier, inc=1, device_id={"dp": dp_peer(k)}, device_id_type=MESH)

    fetch = [pltpu.make_async_copy(ins[i], held[i], loaded.at[i]) for i in range(14)]
    fetch += [pltpu.make_async_copy(ins[i], small[i - 10], indexed.at[i - 10]) for i in (11, 12, 13)]
    for i in (9, 1, 2, 5, 6, 4, 7, 10, 11, 12, 13, 14, 15, 16, 8):
        fetch[i].start()
    for i in (9, 1, 2, 5, 6):
        fetch[i].wait()

    kgain = kg[...]

    for c in range(4):
        x = pre_k[:, c * 128:(c + 1) * 128].astype(F32)
        kv[0, :, c * 128:(c + 1) * 128] = (x * inverse_norm(x) * kgain).astype(BF)
    kv[0, :, 512:] = pre_v[...]
    rows = iota((64, 64), 0)
    spread = (8 * ((rows % 16) // 2) + 2 * (rows // 16) + rows % 2 == iota((64, 64), 1)).astype(F32).astype(BF)
    kv[1, :, :512] = contract(spread, gen_k[...], 1, 0).astype(BF)
    kv[1, :, 512:] = contract(spread, gen_v[...], 1, 0).astype(BF)

    for i in (4, 7):
        fetch[i].wait()
    pl.semaphore_wait(barrier, N - 1 + n_dp - 1)

    def fragment(t):
        rb = pl.multiple_of((t // 8) * 16, 16)
        cb = pl.multiple_of((t % 8) * 128, 128)
        return kv.at[:, pl.ds(rb, 16), pl.ds(cb, 128)]

    def send_1a(t):
        copy(0, fragment(t), r1a.at[me], t).start()

    peers(send_1a)
    r1a[me] = fragment(me)[...]

    def slab(t):
        cols = pl.ds(pl.multiple_of(t * 128, 128), 128)
        q = gen_q[:, cols].astype(F32).reshape(8, 8, 128)
        c = gen_c[:, cols].astype(F32).reshape(8, 8, 128)
        return jnp.concatenate([q, c], axis=1).astype(BF)

    def send_1b(t):
        part = s1b.at[pl.ds(t * 8, 8)]
        part[...] = slab(t)
        copy(1, part, r1b.at[pl.ds(me * 8, 8)], t).start()

    peers(send_1b)
    r1b[pl.ds(me * 8, 8)] = slab(me)

    for i in (8, 10, 11, 12, 13, 14, 15, 16):
        fetch[i].wait()
    qgain = qg[...]
    for i in (0, 3):
        fetch[i].start()
    column = jnp.broadcast_to(dest_row[...], (128, 256)).T
    for half in range(2):
        hit = column == iota((256, 128), 1) + 128 * half
        table[:, half * 128:(half + 1) * 128] = jnp.max(jnp.where(hit, iota((256, 128), 0), 0), axis=0, keepdims=True)
    lookup = pltpu.make_async_copy(table, inv_s, indexed.at[0])
    lookup.start()
    pp = jnp.broadcast_to(pp_row[...].astype(F32), (8, N))
    bp = jnp.broadcast_to(bp_row[...].astype(F32), (8, N))
    pick = (bp_row[...] == iota((N, N), 0)).astype(F32).astype(BF)
    upper = contract(pp.astype(BF), pick, 1, 0)
    spread0 = (iota((N, 512), 0) == iota((N, 512), 1) // 16).astype(F32).astype(BF)
    row0 = (iota((8, 512), 1) % 16).astype(F32)
    spread1 = (iota((N, 1024), 0) == iota((N, 1024), 1) // 32).astype(F32).astype(BF)
    lane1 = iota((8, 1024), 1)
    id0 = contract(pp.astype(BF), spread0, 1, 0) * 16.0 + row0
    parent1 = contract(bp.astype(BF), spread1, 1, 0)
    upper1 = contract(upper.astype(BF), spread1, 1, 0)
    id1 = jnp.where((lane1 // 16) % 2 == 0, parent1, upper1) * 16.0 + (lane1 % 16).astype(F32)
    m0[...] = (iota((512, 512), 0).astype(F32) == id0[:1]).astype(F32).astype(BF)
    m12[...] = (iota((512, 1024), 0).astype(F32) == id1[:1]).astype(F32).astype(BF)
    dest = jnp.broadcast_to(dest_row[...].astype(F32), (8, 256)).astype(BF)
    spread2 = (iota((256, 512), 0) == iota((256, 512), 1) // 2).astype(F32).astype(BF)
    id2 = contract(dest, spread2, 1, 0) * 2.0 + (iota((8, 512), 1) % 2).astype(F32)
    order = (iota((512, 512), 0).astype(F32) == id2[:1]).astype(F32).astype(BF)
    causal[...] = (iota((64, 512), 0) <= iota((64, 512), 1) % 64).astype(F32)

    my_parent = bp_s[0, me]
    my_upper = pp_s[0, my_parent]
    my_above = pp_s[0, me]
    my_root = jnp.where(my_upper >= 0, my_upper, my_parent).astype(F32)
    root = jnp.where(upper >= 0.0, upper, bp)
    member = (root == my_root).astype(F32)
    score = jnp.broadcast_to(rew_row[...].astype(F32), (8, N))
    size = jnp.sum(member, axis=1, keepdims=True)
    center = jnp.sum(member * score, axis=1, keepdims=True) / size
    var = jnp.sum(member * (score - center) ** 2, axis=1, keepdims=True) / size
    adv = ((rew_s[0, me].astype(F32) - center) / jnp.maximum(jnp.sqrt(var), 1.0))[:1]

    await_all(recv.at[0], others(r1a))
    s2a[:, 3] = contract(order, r1a[:, 1].reshape(512, 128), 1, 0).astype(BF).reshape(N, 16, 128)

    def fill_2a(t):
        parent = bp_s[0, t]
        s2a[t, 0] = r1a[jnp.maximum(pp_s[0, t], 0), 0]
        s2a[t, 1] = r1a[parent, 0]
        s2a[t, 2] = r1a[jnp.maximum(pp_s[0, parent], 0), 0]

    def send_2a(t):
        fill_2a(t)
        copy(2, s2a.at[t], r2a.at[me], t).start()

    peers(send_2a)
    fill_2a(me)
    r2a[me] = s2a[me]

    lookup.wait()
    await_all(recv.at[1], others(r1b, 8))

    def send_2b(t):
        for p in range(8):
            s2b[t * 8 + p] = r1b[inv_s[0, t * 8 + p]]
        copy(3, s2b.at[pl.ds(t * 8, 8)], r2b.at[pl.ds(me * 8, 8)], t).start()

    peers(send_2b)
    for p in range(8):
        r2b[me * 8 + p] = r1b[inv_s[0, me * 8 + p]]

    def tiles(ref, at, c):
        return jnp.concatenate([ref[8 * b + c] if at is None else ref[8 * b + c, at] for b in range(4)], axis=0)

    for i in (0, 3):
        fetch[i].wait()
    await_all(recv.at[2], others(r2a))
    g[...] = jnp.zeros((8, 128), F32)
    above = (my_above >= 0).astype(F32)

    @pl.loop(0, 4)
    def _(c):
        col = lambda base, h: pl.ds(pl.multiple_of((base + h) * 128, 128), 128)
        q = jnp.concatenate([pre_q[:, col(8 * c, h)] for h in range(8)], axis=0).astype(F32)
        cot = jnp.concatenate([pre_c[:, col(8 * c, h)] for h in range(8)], axis=0)
        own_k = kv[0, :, col(c, 0)]
        far_k = tiles(r2a, 0, c)
        keys = jnp.concatenate([own_k, far_k], axis=0)
        vals = jnp.concatenate([kv[0, :, col(c, 4)], tiles(r2a, 0, 4 + c)], axis=0)
        mask = jnp.concatenate([causal[...], jnp.full((64, 512), 1.0, F32) * above], axis=0)
        dq, dk, dv, q_term = attend(q, cot, qgain, keys, vals, mask)
        for h in range(8):
            out_q[0:64, col(8 * c, h)] = dq[h * 64:(h + 1) * 64].astype(BF)
        dkp[:, col(c, 0)] = dk[:64]
        dvp[:, col(c, 0)] = dv[:64]
        x = pre_k[:, col(c, 0)].astype(F32)
        k_term = jnp.sum(dk[:64] * x * inverse_norm(x), axis=0, keepdims=True)
        k_term += jnp.sum(dk[64:] * far_k.astype(F32), axis=0, keepdims=True) / kgain
        g[0:1] += q_term
        g[1:2] += k_term
        for b in range(4):
            t0[8 * b + c] = dk[64 + 16 * b:80 + 16 * b].astype(BF)
            t0[8 * b + 4 + c] = dv[64 + 16 * b:80 + 16 * b].astype(BF)

    stores[0].start()
    peers(lambda t: copy(4, t0.at[t], rt0.at[me], t).start())
    rt0[me] = t0[me]

    await_all(send.at[0], others(r1a))
    await_all(send.at[1], others(r1b, 8))
    await_all(send.at[2], others(r2a))

    back = (8 * ((iota((64, 64), 1) % 16) // 2) + 2 * (iota((64, 64), 1) // 16) + iota((64, 64), 1) % 2
            == iota((64, 64), 0)).astype(F32).astype(BF)
    upper_ok = (my_upper >= 0).astype(F32)

    @pl.loop(0, 4)
    def _(step):
        c = lax.rem(lax.div(me, 8) + 6 + lax.div(step + 1, 2) * (1 - 2 * lax.rem(step, 2)), 4)

        mine = c == lax.div(me, 8)

        @pl.when(mine)
        def _():
            await_all(recv.at[8 + c], r2b.at[pl.ds(0, 56)])

        @pl.when(jnp.logical_not(mine))
        def _():
            await_all(recv.at[8 + c], r2b.at[pl.ds(0, 64)])

        col = lambda base, h: pl.ds(pl.multiple_of((base + h) * 128, 128), 128)
        both = r2b[pl.ds(64 * c, 64)].astype(F32)
        q = both[:, :8].reshape(512, 128)
        cot = (both[:, 8:].reshape(512, 128) * adv).astype(BF)
        x = contract(back, tiles(r2a, 3, c), 1, 0)
        r = inverse_norm(x)
        far_k = jnp.concatenate([tiles(r2a, 1, c), tiles(r2a, 2, c)], axis=0)
        keys = jnp.concatenate([(x * r * kgain).astype(BF), far_k], axis=0)
        vals = jnp.concatenate(
            [contract(back, tiles(r2a, 3, 4 + c), 1, 0).astype(BF), tiles(r2a, 1, 4 + c), tiles(r2a, 2, 4 + c)], axis=0
        )
        ones = jnp.full((64, 512), 1.0, F32)
        mask = jnp.concatenate([causal[...], ones, ones * upper_ok], axis=0)
        dq, dk, dv, q_term = attend(q, cot, qgain, keys, vals, mask)
        for h in range(8):
            out_q[64:128, col(8 * c, h)] = dq[h * 64:(h + 1) * 64].astype(BF)
        out_k[64:128, col(c, 0)] = norm_back(x, r, kgain, dk[:64]).astype(BF)
        out_v[64:128, col(c, 0)] = dv[:64].astype(BF)
        k_term = jnp.sum(dk[:64] * x * r, axis=0, keepdims=True)
        k_term += jnp.sum(dk[64:] * far_k.astype(F32), axis=0, keepdims=True) / kgain
        g[0:1] += q_term
        g[1:2] += k_term
        for b in range(4):
            for j in range(2):
                at = 64 + 64 * j + 16 * b
                t12[8 * b + c, j] = dk[at:at + 16].astype(BF)
                t12[8 * b + 4 + c, j] = dv[at:at + 16].astype(BF)
        store_branch(c).start()
        for b in range(8):
            far = (b + 1) // 2 * (1 - 2 * (b % 2))
            t = 4 * lax.rem(lax.div(me, NY) + 12 + far, NZ) + c

            @pl.when(t != me)
            def _():
                copy(5, t12.at[t], rt12.at[me], t).start()

    rt12[me] = t12[me]
    stores[1].start()
    stores[2].start()
    peers(lambda t: copy(6, g, rg.at[me], t).start())
    rg[me] = g[...]

    await_all(recv.at[4], others(rt0))
    total = contract(m0[...], rt0[...].reshape(512, 128), 1, 0)
    await_all(send.at[3], others(r2b, 8))
    await_all(send.at[4], others(rt0))
    await_all(recv.at[5], others(rt12))
    total += contract(m12[...], rt12[...].reshape(1024, 128), 1, 0)
    s4[...] = total.astype(BF).reshape(N, 16, 128)
    peers(lambda t: copy(7, s4.at[t], r4.at[me], t).start())
    r4[me] = s4[me]

    await_all(recv.at[6], others(rg))
    gd[...] = jnp.sum(rg[...], axis=0)

    def dp_copy(k):
        t = dp_peer(k)
        return pltpu.make_async_remote_copy(
            src_ref=gd, dst_ref=rd.at[group], send_sem=dsem.at[0], recv_sem=dsem.at[1],
            device_id={"dp": t}, device_id_type=MESH,
        )

    @pl.loop(1, n_dp)
    def _(k):
        dp_copy(k).start()

    rd[group] = gd[...]

    await_all(recv.at[7], others(r4))
    for c in range(4):
        cols = slice(c * 128, (c + 1) * 128)
        x = pre_k[:, cols].astype(F32)
        dk = dkp[:, cols] + tiles(r4, None, c).astype(F32)
        out_k[0:64, cols] = norm_back(x, inverse_norm(x), kgain, dk).astype(BF)
        out_v[0:64, cols] = (dvp[:, cols] + tiles(r4, None, 4 + c).astype(F32)).astype(BF)

    stores[3].start()
    stores[4].start()

    await_all(dsem.at[1], rd.at[pl.ds(0, n_dp - 1)])

    sums = jnp.sum(rd[...], axis=0)
    out_qg[...] = sums[0:1]
    out_kg[...] = sums[1:2]
    stores[5].start()
    stores[6].start()

    await_all(send.at[5], others(rt12))
    await_all(send.at[6], others(rg))
    await_all(send.at[7], others(r4))
    await_all(dsem.at[0], rd.at[pl.ds(0, n_dp - 1)])
    for each in stores:
        each.wait()

    @pl.loop(0, 4)
    def _(c):
        store_branch(c).wait()


def write_out(*refs):
    src, dst, mid = refs[:5], refs[5:10], refs[10:15]
    loads, stores = refs[15:]
    chunks = [(0, pl.ds(32 * i, 32)) for i in range(4)] + [(1, pl.ds(0, 128)), (2, pl.ds(0, 128))]
    chunks += [(3, pl.ds(0, 1)), (4, pl.ds(0, 1))]
    load = [pltpu.make_async_copy(src[a].at[r], mid[a].at[r], loads.at[n]) for n, (a, r) in enumerate(chunks)]
    store = [pltpu.make_async_copy(mid[a].at[r], dst[a].at[r], stores.at[n]) for n, (a, r) in enumerate(chunks)]
    for each in load:
        each.start()
    for first, then in zip(load, store):
        first.wait()
        then.start()
    for each in store:
        each.wait()


def body(
    pre_q, prefix_keys, prefix_values, pre_cot, gen_q, rollout_keys, rollout_values, gen_cot,
    q_gain, k_gain, piece_dest, prefix_parent, branch_parent, rewards,
):
    n_dp = lax.axis_size("dp")
    hbm = pl.BlockSpec(memory_space=pl.ANY)
    out_q, out_k, out_v, out_qg, out_kg = pl.pallas_call(
        kernel,
        out_shape=(
            jax.ShapeDtypeStruct((128, 4096), BF),
            jax.ShapeDtypeStruct((128, 512), BF),
            jax.ShapeDtypeStruct((128, 512), BF),
            jax.ShapeDtypeStruct((1, 128), F32),
            jax.ShapeDtypeStruct((1, 128), F32),
        ),
        in_specs=[hbm] * 14,
        out_specs=[hbm] * 5,
        scratch_shapes=[
            pltpu.VMEM((64, 4096), BF),
            pltpu.VMEM((64, 512), BF),
            pltpu.VMEM((64, 512), BF),
            pltpu.VMEM((64, 4096), BF),
            pltpu.VMEM((64, 4096), BF),
            pltpu.VMEM((64, 512), BF),
            pltpu.VMEM((64, 512), BF),
            pltpu.VMEM((64, 4096), BF),
            pltpu.VMEM((1, 128), F32),
            pltpu.VMEM((1, 128), F32),
            pltpu.VMEM((1, 256), jnp.int32),
            pltpu.VMEM((1, N), jnp.int32),
            pltpu.VMEM((1, N), jnp.int32),
            pltpu.VMEM((1, N), jnp.int32),
            pltpu.SMEM((1, 256), jnp.int32),
            pltpu.SMEM((1, N), jnp.int32),
            pltpu.SMEM((1, N), jnp.int32),
            pltpu.SMEM((1, N), jnp.int32),
            pltpu.VMEM((1, 256), jnp.int32),
            pltpu.SemaphoreType.DMA((14,)),
            pltpu.SemaphoreType.DMA((4,)),
            pltpu.VMEM((128, 4096), BF),
            pltpu.VMEM((128, 512), BF),
            pltpu.VMEM((128, 512), BF),
            pltpu.VMEM((1, 128), F32),
            pltpu.VMEM((1, 128), F32),
            pltpu.SemaphoreType.DMA((11,)),
            pltpu.VMEM((2, 64, 1024), BF),
            pltpu.VMEM((N, 2, 16, 128), BF),
            pltpu.VMEM((256, 16, 128), BF),
            pltpu.VMEM((256, 16, 128), BF),
            pltpu.VMEM((N, 4, 16, 128), BF),
            pltpu.VMEM((N, 4, 16, 128), BF),
            pltpu.VMEM((256, 16, 128), BF),
            pltpu.VMEM((256, 16, 128), BF),
            pltpu.VMEM((N, 16, 128), BF),
            pltpu.VMEM((N, 16, 128), BF),
            pltpu.VMEM((N, 2, 16, 128), BF),
            pltpu.VMEM((N, 2, 16, 128), BF),
            pltpu.VMEM((N, 16, 128), BF),
            pltpu.VMEM((N, 16, 128), BF),
            pltpu.VMEM((8, 128), F32),
            pltpu.VMEM((N, 8, 128), F32),
            pltpu.VMEM((8, 128), F32),
            pltpu.VMEM((n_dp, 8, 128), F32),
            pltpu.VMEM((512, 512), BF),
            pltpu.VMEM((512, 1024), BF),
            pltpu.VMEM((64, 512), F32),
            pltpu.VMEM((64, 512), F32),
            pltpu.VMEM((64, 512), F32),
            pltpu.SemaphoreType.DMA((8,)),
            pltpu.SemaphoreType.DMA((12,)),
            pltpu.SemaphoreType.DMA((2,)),
        ],
        compiler_params=pltpu.CompilerParams(
            collective_id=0, has_side_effects=True, vmem_limit_bytes=60 * 1024 * 1024
        ),
    )(
        pre_q, prefix_keys, prefix_values, pre_cot, gen_q, rollout_keys, rollout_values, gen_cot,
        q_gain.reshape(1, 128), k_gain.reshape(1, 128),
        piece_dest, prefix_parent, branch_parent, rewards,
    )
    results = (out_q, out_k, out_v, out_qg, out_kg)
    out_q, out_k, out_v, out_qg, out_kg = pl.pallas_call(
        write_out,
        out_shape=tuple(jax.ShapeDtypeStruct(x.shape, x.dtype) for x in results),
        in_specs=[hbm] * 5,
        out_specs=[hbm] * 5,
        scratch_shapes=[pltpu.VMEM(x.shape, x.dtype) for x in results]
        + [pltpu.SemaphoreType.DMA((8,)), pltpu.SemaphoreType.DMA((8,))],
    )(*results)
    return out_q, out_k, out_v, out_qg.reshape(128), out_kg.reshape(128)


def solution(mesh):
    rows = P(("dp", "ctx"), None)
    return jax.shard_map(
        body,
        mesh=mesh,
        in_specs=(rows,) * 8 + (P(), P()) + (P("dp", None),) * 4,
        out_specs=(rows, rows, rows, P(), P()),
        check_vma=False,
    )
```

```python
import math

import jax
import jax.numpy as jnp
from jax import lax
from jax.experimental import pallas as pl
from jax.experimental.pallas import tpu as pltpu
from jax.sharding import PartitionSpec as P

EPSILON = 1e-06
NZ, NY = 8, 4
N = NZ * NY
NEAR = N // 2
BF = jnp.bfloat16
F32 = jnp.float32
MESH = pl.DeviceIdType.MESH
SCALE = 1.0 / math.sqrt(128)


def iota(shape, axis):
    return lax.broadcasted_iota(jnp.int32, shape, axis)


def contract(a, b, da, db):
    return lax.dot_general(a, b, (((da,), (db,)), ((), ())), preferred_element_type=F32)


def inverse_norm(x):
    return lax.rsqrt(jnp.mean(x * x, axis=-1, keepdims=True) + EPSILON)


def norm_back(x, r, gain, upstream):
    scaled = gain * upstream
    inner = jnp.mean(x * scaled, axis=-1, keepdims=True)
    return r * scaled - x * (r * r * r) * inner


def attend(q, cot, gain, keys, vals, mask):
    r = inverse_norm(q)
    qn = (q * r * gain).astype(BF)
    weights = jnp.exp(contract(keys, qn, 1, 1) * SCALE) * mask
    probs = weights * (1.0 / jnp.sum(weights, axis=0, keepdims=True))
    dprob = contract(vals, cot, 1, 1)
    inner = jnp.sum(probs * dprob, axis=0, keepdims=True)
    dscore = (probs * (dprob - inner) * SCALE).astype(BF)
    dq = contract(dscore, keys, 0, 0)
    dk = contract(dscore, qn, 1, 0)
    dv = contract(probs.astype(BF), cot, 1, 0)
    gain_term = jnp.sum(dq * q * r, axis=0, keepdims=True)
    return norm_back(q, r, gain, dq), dk, dv, gain_term


def kernel(*refs):
    ins, outs, rest = refs[:14], refs[14:19], refs[19:]
    held, small, (table, loaded, indexed) = rest[:14], rest[14:18], rest[18:21]
    compute(ins, outs, rest[21:26], held, small, table, loaded, indexed, *rest[26:])


def compute(
    ins, outs, staged, held, small, table, loaded, indexed,
    stored, pkv, rkv, s1a, r1a, s1b, r1b, s2a, r2a, s2b, r2b, t0, rt0, t12, rt12, s4, r4,
    g, rg, gd, rd, m0, m12, dkp, dvp, causal, send, recv, dsem,
):
    pre_q, pre_k, pre_v, pre_c, gen_q, gen_k, gen_v, gen_c, qg, kg, dest_row, pp_row, bp_row, rew_row = held
    inv_s, pp_s, bp_s, rew_s = small
    out_q, out_k, out_v, out_qg, out_kg = staged
    me = lax.axis_index("ctx")
    group = lax.axis_index("dp")
    n_dp = lax.axis_size("dp")

    def peer(k):
        j, m = lax.div(k, NY), lax.rem(k, NY)
        dz = NZ + NZ // 2 + lax.div(j + 1, 2) * (1 - 2 * lax.rem(j, 2))
        dy = NY + NY // 2 + lax.div(m + 1, 2) * (1 - 2 * lax.rem(m, 2))
        return lax.rem(lax.div(me, NY) + dz, NZ) * NY + lax.rem(me + dy, NY)

    def dp_peer(k):
        return lax.rem(group + k, n_dp)

    def copy(stage, src, dst, target):
        arrived = recv.at[8 + lax.div(me, 8)] if stage == 3 else recv.at[stage]
        return pltpu.make_async_remote_copy(
            src_ref=src, dst_ref=dst, send_sem=send.at[stage], recv_sem=arrived,
            device_id={"ctx": target}, device_id_type=MESH,
        )

    def await_all(sem, ref):
        pltpu.make_async_copy(ref, ref, sem).wait()

    def peers(body):
        @pl.loop(0, N - 1)
        def _(k):
            body(peer(k))

    def others(ref, size=1):
        return ref.at[pl.ds(0, (N - 1) * size)]

    def near_others(ref):
        return ref.at[pl.ds(0, NEAR - 1)]

    def near(j, dy, sign):
        dz = 2 - 4 * lax.rem(dy, 2) if j == 0 else (0, 1, -1, 0)[j]
        return lax.rem(lax.div(me, NY) + NZ + sign * dz, NZ) * NY + lax.rem(me + NY + sign * dy, NY)

    def store(i, output, rows):
        return pltpu.make_async_copy(staged[output].at[rows], outs[output].at[rows], stored.at[i])

    upper_half, lower_half = pl.ds(0, 64), pl.ds(64, 64)
    stores = [
        store(0, 0, upper_half), store(1, 1, lower_half), store(2, 2, lower_half),
        store(3, 1, upper_half), store(4, 2, upper_half), store(5, 3, pl.ds(0, 1)), store(6, 4, pl.ds(0, 1)),
    ]

    def store_branch(c):
        at = (lower_half, pl.ds(pl.multiple_of(1024 * c, 128), 1024))
        return pltpu.make_async_copy(staged[0].at[at], outs[0].at[at], stored.at[7 + c])

    barrier = pltpu.get_barrier_semaphore()

    def greet(t):
        pl.semaphore_signal(barrier, inc=1, device_id={"ctx": t}, device_id_type=MESH)

    peers(greet)

    @pl.loop(1, n_dp)
    def _(k):
        pl.semaphore_signal(barrier, inc=1, device_id={"dp": dp_peer(k)}, device_id_type=MESH)

    fetch = [pltpu.make_async_copy(ins[i], held[i], loaded.at[i]) for i in range(14)]
    fetch += [pltpu.make_async_copy(ins[i], small[i - 10], indexed.at[i - 10]) for i in (11, 12, 13)]
    for i in (9, 1, 2, 5, 6, 4, 7, 10, 11, 12, 13, 14, 15, 16, 8):
        fetch[i].start()
    for i in (9, 1, 2, 5, 6):
        fetch[i].wait()

    kgain = kg[...]

    for c in range(4):
        x = pre_k[:, c * 128:(c + 1) * 128].astype(F32)
        pkv[0, :, c * 128:(c + 1) * 128] = (x * inverse_norm(x) * kgain).astype(BF)
    pkv[1] = pre_v[...]
    rows = iota((64, 64), 0)
    spread = (8 * ((rows % 16) // 2) + 2 * (rows // 16) + rows % 2 == iota((64, 64), 1)).astype(F32).astype(BF)
    rkv[:, :512] = contract(spread, gen_k[...], 1, 0).astype(BF)
    rkv[:, 512:] = contract(spread, gen_v[...], 1, 0).astype(BF)

    for i in (4, 7):
        fetch[i].wait()
    pl.semaphore_wait(barrier, N - 1 + n_dp - 1)

    def fill_1a(t):
        rb = pl.multiple_of(lax.rem(lax.div(t, 4), 4) * 16, 16)
        cb = pl.multiple_of(lax.rem(t, 4) * 128, 128)
        s1a[t, 0:2] = pkv[:, pl.ds(rb, 16), pl.ds(cb, 128)]
        rp = pl.multiple_of(lax.rem(t, 4) * 16, 16)
        cr = pl.multiple_of((lax.div(t, 8) + 4 * lax.rem(lax.div(t, 4), 2)) * 128, 128)
        s1a[t, 2] = rkv[pl.ds(rp, 16), pl.ds(cr, 128)]

    def send_1a(t):
        fill_1a(t)
        copy(0, s1a.at[t], r1a.at[me], t).start()

    peers(send_1a)
    fill_1a(me)
    r1a[me] = s1a[me]

    def slab(t):
        cols = pl.ds(pl.multiple_of(t * 128, 128), 128)
        q = gen_q[:, cols].astype(F32).reshape(8, 8, 128)
        c = gen_c[:, cols].astype(F32).reshape(8, 8, 128)
        return jnp.concatenate([q, c], axis=1).astype(BF)

    def send_1b(t):
        part = s1b.at[pl.ds(t * 8, 8)]
        part[...] = slab(t)
        copy(1, part, r1b.at[pl.ds(me * 8, 8)], t).start()

    peers(send_1b)
    r1b[pl.ds(me * 8, 8)] = slab(me)

    for i in (8, 10, 11, 12, 13, 14, 15, 16):
        fetch[i].wait()
    qgain = qg[...]
    for i in (0, 3):
        fetch[i].start()
    column = jnp.broadcast_to(dest_row[...], (128, 256)).T
    for half in range(2):
        hit = column == iota((256, 128), 1) + 128 * half
        table[:, half * 128:(half + 1) * 128] = jnp.max(jnp.where(hit, iota((256, 128), 0), 0), axis=0, keepdims=True)
    lookup = pltpu.make_async_copy(table, inv_s, indexed.at[0])
    lookup.start()
    pp = jnp.broadcast_to(pp_row[...].astype(F32), (8, N))
    bp = jnp.broadcast_to(bp_row[...].astype(F32), (8, N))
    pick = (bp_row[...] == iota((N, N), 0)).astype(F32).astype(BF)
    upper = contract(pp.astype(BF), pick, 1, 0)
    def clients(lane, each):
        k = lane // each
        j, dy = k // NY, k % NY
        dz = jnp.where(j == 0, 2 - 4 * (dy % 2), jnp.where(j == 1, 1, jnp.where(j == 2, -1, 0)))
        at = (lax.div(me, NY) + NZ + dz) % NZ * NY + (me + dy) % NY
        return (iota(lane.shape, 0) == at).astype(F32).astype(BF)

    lane0, lane1 = iota((N, 256), 1), iota((N, 512), 1)
    id0 = contract(pp.astype(BF), clients(lane0, 16), 1, 0) * 16.0 + (lane0 % 16).astype(F32)[:8]
    spread1 = clients(lane1, 32)
    parent1 = contract(bp.astype(BF), spread1, 1, 0)
    upper1 = contract(upper.astype(BF), spread1, 1, 0)
    id1 = jnp.where(((lane1 // 16) % 2 == 0)[:8], parent1, upper1) * 16.0 + (lane1 % 16).astype(F32)[:8]
    m0[...] = (iota((512, 256), 0).astype(F32) == id0[:1]).astype(F32).astype(BF)
    m12[...] = (iota((512, 512), 0).astype(F32) == id1[:1]).astype(F32).astype(BF)
    dest = jnp.broadcast_to(dest_row[...].astype(F32), (8, 256)).astype(BF)
    spread2 = (iota((256, 512), 0) == iota((256, 512), 1) // 2).astype(F32).astype(BF)
    id2 = contract(dest, spread2, 1, 0) * 2.0 + (iota((8, 512), 1) % 2).astype(F32)
    order = (iota((512, 512), 0).astype(F32) == id2[:1]).astype(F32).astype(BF)
    causal[...] = (iota((64, 512), 0) <= iota((64, 512), 1) % 64).astype(F32)

    my_parent = bp_s[0, me]
    my_upper = pp_s[0, my_parent]
    my_above = pp_s[0, me]
    my_root = jnp.where(my_upper >= 0, my_upper, my_parent).astype(F32)
    root = jnp.where(upper >= 0.0, upper, bp)
    member = (root == my_root).astype(F32)
    score = jnp.broadcast_to(rew_row[...].astype(F32), (8, N))
    size = jnp.sum(member, axis=1, keepdims=True)
    center = jnp.sum(member * score, axis=1, keepdims=True) / size
    var = jnp.sum(member * (score - center) ** 2, axis=1, keepdims=True) / size
    adv = ((rew_s[0, me].astype(F32) - center) / jnp.maximum(jnp.sqrt(var), 1.0))[:1]

    await_all(recv.at[0], others(r1a))
    for j in range(4):
        for dy in (2, 1, 3, 0):
            t = near(j, dy, 1)
            k = 4 * j + dy
            parent = bp_s[0, t]
            s2a[k, 0] = r1a[jnp.maximum(pp_s[0, t], 0), 0:2]
            s2a[k, 1] = r1a[parent, 0:2]
            s2a[k, 2] = r1a[jnp.maximum(pp_s[0, parent], 0), 0:2]
            if k != 12:
                copy(2, s2a.at[k], r2a.at[lax.rem(me, NEAR)], t).start()
    r2a[lax.rem(me, NEAR)] = s2a[12]
    s2b[:, 8] = contract(order, r1a[:, 2].reshape(512, 128), 1, 0).astype(BF).reshape(N, 16, 128)

    lookup.wait()
    await_all(recv.at[1], others(r1b, 8))

    def send_2b(t):
        for p in range(8):
            s2b[t, p] = r1b[inv_s[0, t * 8 + p]]
        copy(3, s2b.at[t], r2b.at[me], t).start()

    peers(send_2b)
    for p in range(8):
        r2b[me, p] = r1b[inv_s[0, me * 8 + p]]
    r2b[me, 8] = s2b[me, 8]

    def above_rows(slot, which, c):
        return jnp.concatenate([r2a[4 * b + c, slot, which] for b in range(4)], axis=0)

    def own_rows(first):
        return jnp.concatenate([r2b[first + b, 8] for b in range(4)], axis=0)

    for i in (0, 3):
        fetch[i].wait()
    await_all(recv.at[2], near_others(r2a))
    g[...] = jnp.zeros((8, 128), F32)
    above = (my_above >= 0).astype(F32)

    @pl.loop(0, 4)
    def _(c):
        col = lambda base, h: pl.ds(pl.multiple_of((base + h) * 128, 128), 128)
        q = jnp.concatenate([pre_q[:, col(8 * c, h)] for h in range(8)], axis=0).astype(F32)
        cot = jnp.concatenate([pre_c[:, col(8 * c, h)] for h in range(8)], axis=0)
        own_k = pkv[0, :, col(c, 0)]
        far_k = above_rows(0, 0, c)
        keys = jnp.concatenate([own_k, far_k], axis=0)
        vals = jnp.concatenate([pkv[1, :, col(c, 0)], above_rows(0, 1, c)], axis=0)
        mask = jnp.concatenate([causal[...], jnp.full((64, 512), 1.0, F32) * above], axis=0)
        dq, dk, dv, q_term = attend(q, cot, qgain, keys, vals, mask)
        for h in range(8):
            out_q[0:64, col(8 * c, h)] = dq[h * 64:(h + 1) * 64].astype(BF)
        dkp[:, col(c, 0)] = dk[:64]
        dvp[:, col(c, 0)] = dv[:64]
        x = pre_k[:, col(c, 0)].astype(F32)
        k_term = jnp.sum(dk[:64] * x * inverse_norm(x), axis=0, keepdims=True)
        k_term += jnp.sum(dk[64:] * far_k.astype(F32), axis=0, keepdims=True) / kgain
        g[0:1] += q_term
        g[1:2] += k_term
        for b in range(4):
            t0[4 * b + c, 0] = dk[64 + 16 * b:80 + 16 * b].astype(BF)
            t0[4 * b + c, 1] = dv[64 + 16 * b:80 + 16 * b].astype(BF)

    stores[0].start()
    for j in range(4):
        for dy in (2, 1, 3, 0):
            t = near(j, dy, -1)
            if 4 * j + dy != 12:
                copy(4, t0.at[lax.rem(t, NEAR)], rt0.at[4 * j + dy], t).start()
    rt0[12] = t0[lax.rem(me, NEAR)]

    await_all(send.at[0], others(r1a))
    await_all(send.at[1], others(r1b, 8))
    await_all(send.at[2], near_others(r2a))

    back = (8 * ((iota((64, 64), 1) % 16) // 2) + 2 * (iota((64, 64), 1) // 16) + iota((64, 64), 1) % 2
            == iota((64, 64), 0)).astype(F32).astype(BF)
    upper_ok = (my_upper >= 0).astype(F32)

    @pl.loop(0, 4)
    def _(step):
        c = lax.rem(lax.div(me, 8) + 6 + lax.div(step + 1, 2) * (1 - 2 * lax.rem(step, 2)), 4)

        mine = c == lax.div(me, 8)

        @pl.when(mine)
        def _():
            await_all(recv.at[8 + c], r2b.at[pl.ds(0, 7)])

        @pl.when(jnp.logical_not(mine))
        def _():
            await_all(recv.at[8 + c], r2b.at[pl.ds(0, 8)])

        col = lambda base, h: pl.ds(pl.multiple_of((base + h) * 128, 128), 128)
        both = r2b[pl.ds(8 * c, 8), 0:8].reshape(64, 16, 128).astype(F32)
        q = both[:, :8].reshape(512, 128)
        cot = (both[:, 8:].reshape(512, 128) * adv).astype(BF)
        x = contract(back, own_rows(8 * c), 1, 0)
        r = inverse_norm(x)
        far_k = jnp.concatenate([above_rows(1, 0, c), above_rows(2, 0, c)], axis=0)
        keys = jnp.concatenate([(x * r * kgain).astype(BF), far_k], axis=0)
        vals = jnp.concatenate(
            [contract(back, own_rows(8 * c + 4), 1, 0).astype(BF), above_rows(1, 1, c), above_rows(2, 1, c)], axis=0
        )
        ones = jnp.full((64, 512), 1.0, F32)
        mask = jnp.concatenate([causal[...], ones, ones * upper_ok], axis=0)
        dq, dk, dv, q_term = attend(q, cot, qgain, keys, vals, mask)
        for h in range(8):
            out_q[64:128, col(8 * c, h)] = dq[h * 64:(h + 1) * 64].astype(BF)
        out_k[64:128, col(c, 0)] = norm_back(x, r, kgain, dk[:64]).astype(BF)
        out_v[64:128, col(c, 0)] = dv[:64].astype(BF)
        k_term = jnp.sum(dk[:64] * x * r, axis=0, keepdims=True)
        k_term += jnp.sum(dk[64:] * far_k.astype(F32), axis=0, keepdims=True) / kgain
        g[0:1] += q_term
        g[1:2] += k_term
        for b in range(4):
            for j in range(2):
                at = 64 + 64 * j + 16 * b
                t12[4 * b + c, j, 0] = dk[at:at + 16].astype(BF)
                t12[4 * b + c, j, 1] = dv[at:at + 16].astype(BF)
        store_branch(c).start()
        dy = lax.rem(me + 4 - c, NY)
        for j in range(4):
            t = near(j, dy, -1)

            @pl.when(t != me)
            def _():
                copy(5, t12.at[lax.rem(t, NEAR)], rt12.at[4 * j + dy], t).start()

    rt12[12] = t12[lax.rem(me, NEAR)]
    stores[1].start()
    stores[2].start()
    peers(lambda t: copy(6, g, rg.at[me], t).start())
    rg[me] = g[...]

    def columns(first, second, rows):
        return jnp.concatenate([first.reshape(rows, 128), second.reshape(rows, 128)], axis=1)

    await_all(recv.at[4], near_others(rt0))
    total = contract(m0[...], columns(rt0[:, 0], rt0[:, 1], 256), 1, 0)
    await_all(send.at[3], others(r2b))
    await_all(send.at[4], near_others(rt0))
    await_all(recv.at[5], near_others(rt12))
    total += contract(m12[...], columns(rt12[:, :, 0], rt12[:, :, 1], 512), 1, 0)
    s4[:, 0] = total[:, :128].astype(BF).reshape(N, 16, 128)
    s4[:, 1] = total[:, 128:].astype(BF).reshape(N, 16, 128)
    peers(lambda t: copy(7, s4.at[t], r4.at[me], t).start())
    r4[me] = s4[me]

    await_all(recv.at[6], others(rg))
    gd[...] = jnp.sum(rg[...], axis=0)

    def dp_copy(k):
        t = dp_peer(k)
        return pltpu.make_async_remote_copy(
            src_ref=gd, dst_ref=rd.at[group], send_sem=dsem.at[0], recv_sem=dsem.at[1],
            device_id={"dp": t}, device_id_type=MESH,
        )

    @pl.loop(1, n_dp)
    def _(k):
        dp_copy(k).start()

    rd[group] = gd[...]

    await_all(recv.at[7], others(r4))
    def far_rows(which, c):
        pairs = [r4[4 * b + c, which].astype(F32) + r4[NEAR + 4 * b + c, which].astype(F32) for b in range(4)]
        return jnp.concatenate(pairs, axis=0)

    for c in range(4):
        cols = slice(c * 128, (c + 1) * 128)
        x = pre_k[:, cols].astype(F32)
        dk = dkp[:, cols] + far_rows(0, c)
        out_k[0:64, cols] = norm_back(x, inverse_norm(x), kgain, dk).astype(BF)
        out_v[0:64, cols] = (dvp[:, cols] + far_rows(1, c)).astype(BF)

    stores[3].start()
    stores[4].start()

    await_all(dsem.at[1], rd.at[pl.ds(0, n_dp - 1)])

    sums = jnp.sum(rd[...], axis=0)
    out_qg[...] = sums[0:1]
    out_kg[...] = sums[1:2]
    stores[5].start()
    stores[6].start()

    await_all(send.at[5], near_others(rt12))
    await_all(send.at[6], others(rg))
    await_all(send.at[7], others(r4))
    await_all(dsem.at[0], rd.at[pl.ds(0, n_dp - 1)])
    for each in stores:
        each.wait()

    @pl.loop(0, 4)
    def _(c):
        store_branch(c).wait()


def write_out(*refs):
    src, dst, mid = refs[:5], refs[5:10], refs[10:15]
    loads, stores = refs[15:]
    chunks = [(0, pl.ds(32 * i, 32)) for i in range(4)] + [(1, pl.ds(0, 128)), (2, pl.ds(0, 128))]
    chunks += [(3, pl.ds(0, 1)), (4, pl.ds(0, 1))]
    load = [pltpu.make_async_copy(src[a].at[r], mid[a].at[r], loads.at[n]) for n, (a, r) in enumerate(chunks)]
    store = [pltpu.make_async_copy(mid[a].at[r], dst[a].at[r], stores.at[n]) for n, (a, r) in enumerate(chunks)]
    for each in load:
        each.start()
    for first, then in zip(load, store):
        first.wait()
        then.start()
    for each in store:
        each.wait()


def body(
    pre_q, prefix_keys, prefix_values, pre_cot, gen_q, rollout_keys, rollout_values, gen_cot,
    q_gain, k_gain, piece_dest, prefix_parent, branch_parent, rewards,
):
    n_dp = lax.axis_size("dp")
    hbm = pl.BlockSpec(memory_space=pl.ANY)
    out_q, out_k, out_v, out_qg, out_kg = pl.pallas_call(
        kernel,
        out_shape=(
            jax.ShapeDtypeStruct((128, 4096), BF),
            jax.ShapeDtypeStruct((128, 512), BF),
            jax.ShapeDtypeStruct((128, 512), BF),
            jax.ShapeDtypeStruct((1, 128), F32),
            jax.ShapeDtypeStruct((1, 128), F32),
        ),
        in_specs=[hbm] * 14,
        out_specs=[hbm] * 5,
        scratch_shapes=[
            pltpu.VMEM((64, 4096), BF),
            pltpu.VMEM((64, 512), BF),
            pltpu.VMEM((64, 512), BF),
            pltpu.VMEM((64, 4096), BF),
            pltpu.VMEM((64, 4096), BF),
            pltpu.VMEM((64, 512), BF),
            pltpu.VMEM((64, 512), BF),
            pltpu.VMEM((64, 4096), BF),
            pltpu.VMEM((1, 128), F32),
            pltpu.VMEM((1, 128), F32),
            pltpu.VMEM((1, 256), jnp.int32),
            pltpu.VMEM((1, N), jnp.int32),
            pltpu.VMEM((1, N), jnp.int32),
            pltpu.VMEM((1, N), jnp.int32),
            pltpu.SMEM((1, 256), jnp.int32),
            pltpu.SMEM((1, N), jnp.int32),
            pltpu.SMEM((1, N), jnp.int32),
            pltpu.SMEM((1, N), jnp.int32),
            pltpu.VMEM((1, 256), jnp.int32),
            pltpu.SemaphoreType.DMA((14,)),
            pltpu.SemaphoreType.DMA((4,)),
            pltpu.VMEM((128, 4096), BF),
            pltpu.VMEM((128, 512), BF),
            pltpu.VMEM((128, 512), BF),
            pltpu.VMEM((1, 128), F32),
            pltpu.VMEM((1, 128), F32),
            pltpu.SemaphoreType.DMA((11,)),
            pltpu.VMEM((2, 64, 512), BF),
            pltpu.VMEM((64, 1024), BF),
            pltpu.VMEM((N, 3, 16, 128), BF),
            pltpu.VMEM((N, 3, 16, 128), BF),
            pltpu.VMEM((256, 16, 128), BF),
            pltpu.VMEM((256, 16, 128), BF),
            pltpu.VMEM((NEAR, 3, 2, 16, 128), BF),
            pltpu.VMEM((NEAR, 3, 2, 16, 128), BF),
            pltpu.VMEM((N, 9, 16, 128), BF),
            pltpu.VMEM((N, 9, 16, 128), BF),
            pltpu.VMEM((NEAR, 2, 16, 128), BF),
            pltpu.VMEM((NEAR, 2, 16, 128), BF),
            pltpu.VMEM((NEAR, 2, 2, 16, 128), BF),
            pltpu.VMEM((NEAR, 2, 2, 16, 128), BF),
            pltpu.VMEM((N, 2, 16, 128), BF),
            pltpu.VMEM((N, 2, 16, 128), BF),
            pltpu.VMEM((8, 128), F32),
            pltpu.VMEM((N, 8, 128), F32),
            pltpu.VMEM((8, 128), F32),
            pltpu.VMEM((n_dp, 8, 128), F32),
            pltpu.VMEM((512, 256), BF),
            pltpu.VMEM((512, 512), BF),
            pltpu.VMEM((64, 512), F32),
            pltpu.VMEM((64, 512), F32),
            pltpu.VMEM((64, 512), F32),
            pltpu.SemaphoreType.DMA((8,)),
            pltpu.SemaphoreType.DMA((12,)),
            pltpu.SemaphoreType.DMA((2,)),
        ],
        compiler_params=pltpu.CompilerParams(
            collective_id=0, has_side_effects=True, vmem_limit_bytes=60 * 1024 * 1024
        ),
    )(
        pre_q, prefix_keys, prefix_values, pre_cot, gen_q, rollout_keys, rollout_values, gen_cot,
        q_gain.reshape(1, 128), k_gain.reshape(1, 128),
        piece_dest, prefix_parent, branch_parent, rewards,
    )
    results = (out_q, out_k, out_v, out_qg, out_kg)
    out_q, out_k, out_v, out_qg, out_kg = pl.pallas_call(
        write_out,
        out_shape=tuple(jax.ShapeDtypeStruct(x.shape, x.dtype) for x in results),
        in_specs=[hbm] * 5,
        out_specs=[hbm] * 5,
        scratch_shapes=[pltpu.VMEM(x.shape, x.dtype) for x in results]
        + [pltpu.SemaphoreType.DMA((8,)), pltpu.SemaphoreType.DMA((8,))],
    )(*results)
    return out_q, out_k, out_v, out_qg.reshape(128), out_kg.reshape(128)


def solution(mesh):
    rows = P(("dp", "ctx"), None)
    return jax.shard_map(
        body,
        mesh=mesh,
        in_specs=(rows,) * 8 + (P(), P()) + (P("dp", None),) * 4,
        out_specs=(rows, rows, rows, P(), P()),
        check_vma=False,
    )
```

```python
import math

import jax
import jax.numpy as jnp
from jax import lax
from jax.experimental import pallas as pl
from jax.experimental.pallas import tpu as pltpu
from jax.sharding import PartitionSpec as P

EPSILON = 1e-06
NZ, NY = 8, 4
N = NZ * NY
NEAR = N // 2
BF = jnp.bfloat16
F32 = jnp.float32
MESH = pl.DeviceIdType.MESH
SCALE = 1.0 / math.sqrt(128)


def iota(shape, axis):
    return lax.broadcasted_iota(jnp.int32, shape, axis)


def contract(a, b, da, db):
    return lax.dot_general(a, b, (((da,), (db,)), ((), ())), preferred_element_type=F32)


def inverse_norm(x):
    return lax.rsqrt(jnp.mean(x * x, axis=-1, keepdims=True) + EPSILON)


def norm_back(x, r, gain, upstream):
    scaled = gain * upstream
    inner = jnp.mean(x * scaled, axis=-1, keepdims=True)
    return r * scaled - x * (r * r * r) * inner


def attend_keys(q, cot, gain, keys, vals, mask):
    qn = (q * inverse_norm(q) * gain).astype(BF)
    weights = jnp.exp(contract(keys, qn, 1, 1) * SCALE) * mask
    probs = weights * (1.0 / jnp.sum(weights, axis=0, keepdims=True))
    dprob = contract(vals, cot, 1, 1)
    inner = jnp.sum(probs * dprob, axis=0, keepdims=True)
    dscore = (probs * (dprob - inner) * SCALE).astype(BF)
    return dscore, contract(dscore, qn, 1, 0), contract(probs.astype(BF), cot, 1, 0)


def attend_queries(q, gain, keys, dscore):
    return norm_back(q, inverse_norm(q), gain, contract(dscore, keys, 0, 0))


def kernel(*refs):
    ins, outs, rest = refs[:14], refs[14:19], refs[19:]
    held, small, (table, loaded, indexed) = rest[:14], rest[14:18], rest[18:21]
    compute(ins, outs, rest[21:26], held, small, table, loaded, indexed, *rest[26:])


def compute(
    ins, outs, staged, held, small, table, loaded, indexed,
    stored, dscores, allkeys, branch_x, dkb, pkv, rkv, s1a, r1a, s1b, r1b, s2a, r2a, s2b, r2b, t0, rt0, t12, rt12, s4, r4,
    g, rg, gd, rd, m0, m12, dkp, dvp, causal, send, recv, dsem,
):
    pre_q, pre_k, pre_v, pre_c, gen_q, gen_k, gen_v, gen_c, qg, kg, dest_row, pp_row, bp_row, rew_row = held
    inv_s, pp_s, bp_s, rew_s = small
    out_q, out_k, out_v, out_qg, out_kg = staged
    me = lax.axis_index("ctx")
    group = lax.axis_index("dp")
    n_dp = lax.axis_size("dp")

    def peer(k):
        j, m = lax.div(k, NY), lax.rem(k, NY)
        dz = NZ + NZ // 2 + lax.div(j + 1, 2) * (1 - 2 * lax.rem(j, 2))
        dy = NY + NY // 2 + lax.div(m + 1, 2) * (1 - 2 * lax.rem(m, 2))
        return lax.rem(lax.div(me, NY) + dz, NZ) * NY + lax.rem(me + dy, NY)

    def dp_peer(k):
        return lax.rem(group + k, n_dp)

    def copy(stage, src, dst, target):
        arrived = recv.at[8 + lax.div(me, 8)] if stage == 3 else recv.at[stage]
        return pltpu.make_async_remote_copy(
            src_ref=src, dst_ref=dst, send_sem=send.at[stage], recv_sem=arrived,
            device_id={"ctx": target}, device_id_type=MESH,
        )

    def await_all(sem, ref):
        pltpu.make_async_copy(ref, ref, sem).wait()

    def peers(body):
        @pl.loop(0, N - 1)
        def _(k):
            body(peer(k))

    def others(ref, size=1):
        return ref.at[pl.ds(0, (N - 1) * size)]

    def near_others(ref):
        return ref.at[pl.ds(0, NEAR - 1)]

    def near(j, dy, sign):
        dz = 2 - 4 * lax.rem(dy, 2) if j == 0 else (0, 1, -1, 0)[j]
        return lax.rem(lax.div(me, NY) + NZ + sign * dz, NZ) * NY + lax.rem(me + NY + sign * dy, NY)

    def store(i, output, rows):
        return pltpu.make_async_copy(staged[output].at[rows], outs[output].at[rows], stored.at[i])

    upper_half, lower_half = pl.ds(0, 64), pl.ds(64, 64)
    stores = [
        store(0, 0, upper_half), store(1, 1, lower_half), store(2, 2, lower_half),
        store(3, 1, upper_half), store(4, 2, upper_half), store(5, 3, pl.ds(0, 1)), store(6, 4, pl.ds(0, 1)),
    ]

    def store_branch(c):
        at = (lower_half, pl.ds(pl.multiple_of(1024 * c, 128), 1024))
        return pltpu.make_async_copy(staged[0].at[at], outs[0].at[at], stored.at[7 + c])

    barrier = pltpu.get_barrier_semaphore()

    def greet(t):
        pl.semaphore_signal(barrier, inc=1, device_id={"ctx": t}, device_id_type=MESH)

    peers(greet)

    @pl.loop(1, n_dp)
    def _(k):
        pl.semaphore_signal(barrier, inc=1, device_id={"dp": dp_peer(k)}, device_id_type=MESH)

    fetch = [pltpu.make_async_copy(ins[i], held[i], loaded.at[i]) for i in range(14)]
    fetch += [pltpu.make_async_copy(ins[i], small[i - 10], indexed.at[i - 10]) for i in (11, 12, 13)]
    for i in (9, 1, 2, 5, 6, 4, 7, 10, 11, 12, 13, 14, 15, 16, 8):
        fetch[i].start()
    for i in (9, 1, 2, 5, 6):
        fetch[i].wait()

    kgain = kg[...]

    for c in range(4):
        x = pre_k[:, c * 128:(c + 1) * 128].astype(F32)
        pkv[0, :, c * 128:(c + 1) * 128] = (x * inverse_norm(x) * kgain).astype(BF)
    pkv[1] = pre_v[...]
    rows = iota((64, 64), 0)
    spread = (8 * ((rows % 16) // 2) + 2 * (rows // 16) + rows % 2 == iota((64, 64), 1)).astype(F32).astype(BF)
    rkv[:, :512] = contract(spread, gen_k[...], 1, 0).astype(BF)
    rkv[:, 512:] = contract(spread, gen_v[...], 1, 0).astype(BF)

    for i in (4, 7):
        fetch[i].wait()
    pl.semaphore_wait(barrier, N - 1 + n_dp - 1)

    def fill_1a(t):
        rb = pl.multiple_of(lax.rem(lax.div(t, 4), 4) * 16, 16)
        cb = pl.multiple_of(lax.rem(t, 4) * 128, 128)
        s1a[t, 0:2] = pkv[:, pl.ds(rb, 16), pl.ds(cb, 128)]
        rp = pl.multiple_of(lax.rem(t, 4) * 16, 16)
        cr = pl.multiple_of((lax.div(t, 8) + 4 * lax.rem(lax.div(t, 4), 2)) * 128, 128)
        s1a[t, 2] = rkv[pl.ds(rp, 16), pl.ds(cr, 128)]

    def send_1a(t):
        fill_1a(t)
        copy(0, s1a.at[t], r1a.at[me], t).start()

    peers(send_1a)
    fill_1a(me)
    r1a[me] = s1a[me]

    def slab(t):
        cols = pl.ds(pl.multiple_of(t * 128, 128), 128)
        q = gen_q[:, cols].astype(F32).reshape(8, 8, 128)
        c = gen_c[:, cols].astype(F32).reshape(8, 8, 128)
        return jnp.concatenate([q, c], axis=1).astype(BF)

    def send_1b(t):
        part = s1b.at[pl.ds(t * 8, 8)]
        part[...] = slab(t)
        copy(1, part, r1b.at[pl.ds(me * 8, 8)], t).start()

    peers(send_1b)
    r1b[pl.ds(me * 8, 8)] = slab(me)

    for i in (8, 10, 11, 12, 13, 14, 15, 16):
        fetch[i].wait()
    qgain = qg[...]
    for i in (0, 3):
        fetch[i].start()
    column = jnp.broadcast_to(dest_row[...], (128, 256)).T
    for half in range(2):
        hit = column == iota((256, 128), 1) + 128 * half
        table[:, half * 128:(half + 1) * 128] = jnp.max(jnp.where(hit, iota((256, 128), 0), 0), axis=0, keepdims=True)
    lookup = pltpu.make_async_copy(table, inv_s, indexed.at[0])
    lookup.start()
    pp = jnp.broadcast_to(pp_row[...].astype(F32), (8, N))
    bp = jnp.broadcast_to(bp_row[...].astype(F32), (8, N))
    pick = (bp_row[...] == iota((N, N), 0)).astype(F32).astype(BF)
    upper = contract(pp.astype(BF), pick, 1, 0)
    def clients(lane, each):
        k = lane // each
        j, dy = k // NY, k % NY
        dz = jnp.where(j == 0, 2 - 4 * (dy % 2), jnp.where(j == 1, 1, jnp.where(j == 2, -1, 0)))
        at = (lax.div(me, NY) + NZ + dz) % NZ * NY + (me + dy) % NY
        return (iota(lane.shape, 0) == at).astype(F32).astype(BF)

    lane0, lane1 = iota((N, 256), 1), iota((N, 512), 1)
    id0 = contract(pp.astype(BF), clients(lane0, 16), 1, 0) * 16.0 + (lane0 % 16).astype(F32)[:8]
    spread1 = clients(lane1, 32)
    parent1 = contract(bp.astype(BF), spread1, 1, 0)
    upper1 = contract(upper.astype(BF), spread1, 1, 0)
    id1 = jnp.where(((lane1 // 16) % 2 == 0)[:8], parent1, upper1) * 16.0 + (lane1 % 16).astype(F32)[:8]
    m0[...] = (iota((512, 256), 0).astype(F32) == id0[:1]).astype(F32).astype(BF)
    m12[...] = (iota((512, 512), 0).astype(F32) == id1[:1]).astype(F32).astype(BF)
    dest = jnp.broadcast_to(dest_row[...].astype(F32), (8, 256)).astype(BF)
    spread2 = (iota((256, 512), 0) == iota((256, 512), 1) // 2).astype(F32).astype(BF)
    id2 = contract(dest, spread2, 1, 0) * 2.0 + (iota((8, 512), 1) % 2).astype(F32)
    order = (iota((512, 512), 0).astype(F32) == id2[:1]).astype(F32).astype(BF)
    causal[...] = (iota((64, 512), 0) <= iota((64, 512), 1) % 64).astype(F32)

    my_parent = bp_s[0, me]
    my_upper = pp_s[0, my_parent]
    my_above = pp_s[0, me]
    my_root = jnp.where(my_upper >= 0, my_upper, my_parent).astype(F32)
    root = jnp.where(upper >= 0.0, upper, bp)
    member = (root == my_root).astype(F32)
    score = jnp.broadcast_to(rew_row[...].astype(F32), (8, N))
    size = jnp.sum(member, axis=1, keepdims=True)
    center = jnp.sum(member * score, axis=1, keepdims=True) / size
    var = jnp.sum(member * (score - center) ** 2, axis=1, keepdims=True) / size
    adv = ((rew_s[0, me].astype(F32) - center) / jnp.maximum(jnp.sqrt(var), 1.0))[:1]

    await_all(recv.at[0], others(r1a))
    for j in range(4):
        for dy in (2, 1, 3, 0):
            t = near(j, dy, 1)
            k = 4 * j + dy
            parent = bp_s[0, t]
            s2a[k, 0] = r1a[jnp.maximum(pp_s[0, t], 0), 0:2]
            s2a[k, 1] = r1a[parent, 0:2]
            s2a[k, 2] = r1a[jnp.maximum(pp_s[0, parent], 0), 0:2]
            if k != 12:
                copy(2, s2a.at[k], r2a.at[lax.rem(me, NEAR)], t).start()
    r2a[lax.rem(me, NEAR)] = s2a[12]
    s2b[:, 8] = contract(order, r1a[:, 2].reshape(512, 128), 1, 0).astype(BF).reshape(N, 16, 128)

    lookup.wait()
    await_all(recv.at[1], others(r1b, 8))

    def send_2b(t):
        for p in range(8):
            s2b[t, p] = r1b[inv_s[0, t * 8 + p]]
        copy(3, s2b.at[t], r2b.at[me], t).start()

    peers(send_2b)
    for p in range(8):
        r2b[me, p] = r1b[inv_s[0, me * 8 + p]]
    r2b[me, 8] = s2b[me, 8]

    def above_rows(slot, which, c):
        return jnp.concatenate([r2a[4 * b + c, slot, which] for b in range(4)], axis=0)

    def own_rows(first):
        return jnp.concatenate([r2b[first + b, 8] for b in range(4)], axis=0)

    for i in (0, 3):
        fetch[i].wait()
    await_all(recv.at[2], near_others(r2a))
    g[...] = jnp.zeros((1, 128), F32)
    above = (my_above >= 0).astype(F32)

    @pl.loop(0, 4)
    def _(c):
        col = lambda base, h: pl.ds(pl.multiple_of((base + h) * 128, 128), 128)
        q = jnp.concatenate([pre_q[:, col(8 * c, h)] for h in range(8)], axis=0).astype(F32)
        cot = jnp.concatenate([pre_c[:, col(8 * c, h)] for h in range(8)], axis=0)
        own_k = pkv[0, :, col(c, 0)]
        far_k = above_rows(0, 0, c)
        keys = jnp.concatenate([own_k, far_k], axis=0)
        vals = jnp.concatenate([pkv[1, :, col(c, 0)], above_rows(0, 1, c)], axis=0)
        mask = jnp.concatenate([causal[...], jnp.full((64, 512), 1.0, F32) * above], axis=0)
        dscore, dk, dv = attend_keys(q, cot, qgain, keys, vals, mask)
        dq = attend_queries(q, qgain, keys, dscore)
        for h in range(8):
            out_q[0:64, col(8 * c, h)] = dq[h * 64:(h + 1) * 64].astype(BF)
        dkp[:, col(c, 0)] = dk[:64]
        dvp[:, col(c, 0)] = dv[:64]
        g[...] += jnp.sum(dk * keys.astype(F32), axis=0, keepdims=True)
        for b in range(4):
            t0[4 * b + c, 0] = dk[64 + 16 * b:80 + 16 * b].astype(BF)
            t0[4 * b + c, 1] = dv[64 + 16 * b:80 + 16 * b].astype(BF)

    stores[0].start()
    for j in range(4):
        for dy in (2, 1, 3, 0):
            t = near(j, dy, -1)
            if 4 * j + dy != 12:
                copy(4, t0.at[lax.rem(t, NEAR)], rt0.at[4 * j + dy], t).start()
    rt0[12] = t0[lax.rem(me, NEAR)]

    await_all(send.at[0], others(r1a))
    await_all(send.at[1], others(r1b, 8))
    await_all(send.at[2], near_others(r2a))

    back = (8 * ((iota((64, 64), 1) % 16) // 2) + 2 * (iota((64, 64), 1) // 16) + iota((64, 64), 1) % 2
            == iota((64, 64), 0)).astype(F32).astype(BF)
    upper_ok = (my_upper >= 0).astype(F32)

    @pl.loop(0, 4)
    def _(step):
        c = lax.rem(lax.div(me, 8) + 6 + lax.div(step + 1, 2) * (1 - 2 * lax.rem(step, 2)), 4)

        mine = c == lax.div(me, 8)

        @pl.when(mine)
        def _():
            await_all(recv.at[8 + c], r2b.at[pl.ds(0, 7)])

        @pl.when(jnp.logical_not(mine))
        def _():
            await_all(recv.at[8 + c], r2b.at[pl.ds(0, 8)])

        col = lambda base, h: pl.ds(pl.multiple_of((base + h) * 128, 128), 128)
        both = r2b[pl.ds(8 * c, 8), 0:8].reshape(64, 16, 128).astype(F32)
        q = both[:, :8].reshape(512, 128)
        cot = (both[:, 8:].reshape(512, 128) * adv).astype(BF)
        x = contract(back, own_rows(8 * c), 1, 0)
        r = inverse_norm(x)
        far_k = jnp.concatenate([above_rows(1, 0, c), above_rows(2, 0, c)], axis=0)
        keys = jnp.concatenate([(x * r * kgain).astype(BF), far_k], axis=0)
        vals = jnp.concatenate(
            [contract(back, own_rows(8 * c + 4), 1, 0).astype(BF), above_rows(1, 1, c), above_rows(2, 1, c)], axis=0
        )
        ones = jnp.full((64, 512), 1.0, F32)
        mask = jnp.concatenate([causal[...], ones, ones * upper_ok], axis=0)
        dscore, dk, dv = attend_keys(q, cot, qgain, keys, vals, mask)
        for b in range(4):
            for j in range(2):
                at = 64 + 64 * j + 16 * b
                t12[4 * b + c, j, 0] = dk[at:at + 16].astype(BF)
                t12[4 * b + c, j, 1] = dv[at:at + 16].astype(BF)
        dy = lax.rem(me + 4 - c, NY)
        for j in range(4):
            t = near(j, dy, -1)

            @pl.when(t != me)
            def _():
                copy(5, t12.at[lax.rem(t, NEAR)], rt12.at[4 * j + dy], t).start()

        out_v[64:128, col(c, 0)] = dv[:64].astype(BF)
        dscores[c] = dscore
        allkeys[c] = keys
        branch_x[:, col(c, 0)] = x
        dkb[:, col(c, 0)] = dk[:64]
        g[...] += jnp.sum(dk * keys.astype(F32), axis=0, keepdims=True)

    rt12[12] = t12[lax.rem(me, NEAR)]

    peers(lambda t: copy(6, g, rg.at[me], t).start())
    rg[me] = g[...]

    @pl.loop(0, 4)
    def _(c):
        col = lambda base, h: pl.ds(pl.multiple_of((base + h) * 128, 128), 128)
        q = r2b[pl.ds(8 * c, 8), 0:8].reshape(64, 16, 128).astype(F32)[:, :8].reshape(512, 128)
        dq = attend_queries(q, qgain, allkeys[c], dscores[c])
        for h in range(8):
            out_q[64:128, col(8 * c, h)] = dq[h * 64:(h + 1) * 64].astype(BF)
        store_branch(c).start()
        x, dk = branch_x[:, col(c, 0)], dkb[:, col(c, 0)]
        out_k[64:128, col(c, 0)] = norm_back(x, inverse_norm(x), kgain, dk).astype(BF)

    stores[1].start()
    stores[2].start()

    def columns(first, second, rows):
        return jnp.concatenate([first.reshape(rows, 128), second.reshape(rows, 128)], axis=1)

    await_all(recv.at[4], near_others(rt0))
    total = contract(m0[...], columns(rt0[:, 0], rt0[:, 1], 256), 1, 0)
    await_all(send.at[3], others(r2b))
    await_all(send.at[4], near_others(rt0))
    await_all(recv.at[5], near_others(rt12))
    total += contract(m12[...], columns(rt12[:, :, 0], rt12[:, :, 1], 512), 1, 0)
    s4[:, 0] = total[:, :128].astype(BF).reshape(N, 16, 128)
    s4[:, 1] = total[:, 128:].astype(BF).reshape(N, 16, 128)

    @pl.loop(0, N)
    def _(t):
        @pl.when(t != me)
        def _():
            copy(7, s4.at[t], r4.at[me], t).start()

    r4[me] = s4[me]

    await_all(recv.at[6], others(rg))
    gd[...] = jnp.sum(rg[...], axis=0)

    def dp_copy(k):
        t = dp_peer(k)
        return pltpu.make_async_remote_copy(
            src_ref=gd, dst_ref=rd.at[group], send_sem=dsem.at[0], recv_sem=dsem.at[1],
            device_id={"dp": t}, device_id_type=MESH,
        )

    @pl.loop(1, n_dp)
    def _(k):
        dp_copy(k).start()

    rd[group] = gd[...]

    await_all(recv.at[7], others(r4))
    def far_rows(which, c):
        pairs = [r4[4 * b + c, which].astype(F32) + r4[NEAR + 4 * b + c, which].astype(F32) for b in range(4)]
        return jnp.concatenate(pairs, axis=0)

    for c in range(4):
        cols = slice(c * 128, (c + 1) * 128)
        x = pre_k[:, cols].astype(F32)
        dk = dkp[:, cols] + far_rows(0, c)
        out_k[0:64, cols] = norm_back(x, inverse_norm(x), kgain, dk).astype(BF)
        out_v[0:64, cols] = (dvp[:, cols] + far_rows(1, c)).astype(BF)

    stores[3].start()
    stores[4].start()

    await_all(dsem.at[1], rd.at[pl.ds(0, n_dp - 1)])

    sums = jnp.sum(rd[...], axis=0)
    out_qg[...] = sums / qgain
    out_kg[...] = sums / kgain
    stores[5].start()
    stores[6].start()

    await_all(send.at[5], near_others(rt12))
    await_all(send.at[6], others(rg))
    await_all(send.at[7], others(r4))
    await_all(dsem.at[0], rd.at[pl.ds(0, n_dp - 1)])
    for each in stores:
        each.wait()

    @pl.loop(0, 4)
    def _(c):
        store_branch(c).wait()


def write_out(*refs):
    src, dst, mid = refs[:5], refs[5:10], refs[10:15]
    loads, stores = refs[15:]
    chunks = [(0, pl.ds(32 * i, 32)) for i in range(4)] + [(1, pl.ds(0, 128)), (2, pl.ds(0, 128))]
    chunks += [(3, pl.ds(0, 1)), (4, pl.ds(0, 1))]
    load = [pltpu.make_async_copy(src[a].at[r], mid[a].at[r], loads.at[n]) for n, (a, r) in enumerate(chunks)]
    store = [pltpu.make_async_copy(mid[a].at[r], dst[a].at[r], stores.at[n]) for n, (a, r) in enumerate(chunks)]
    for each in load:
        each.start()
    for first, then in zip(load, store):
        first.wait()
        then.start()
    for each in store:
        each.wait()


def body(
    pre_q, prefix_keys, prefix_values, pre_cot, gen_q, rollout_keys, rollout_values, gen_cot,
    q_gain, k_gain, piece_dest, prefix_parent, branch_parent, rewards,
):
    n_dp = lax.axis_size("dp")
    hbm = pl.BlockSpec(memory_space=pl.ANY)
    out_q, out_k, out_v, out_qg, out_kg = pl.pallas_call(
        kernel,
        out_shape=(
            jax.ShapeDtypeStruct((128, 4096), BF),
            jax.ShapeDtypeStruct((128, 512), BF),
            jax.ShapeDtypeStruct((128, 512), BF),
            jax.ShapeDtypeStruct((1, 128), F32),
            jax.ShapeDtypeStruct((1, 128), F32),
        ),
        in_specs=[hbm] * 14,
        out_specs=[hbm] * 5,
        scratch_shapes=[
            pltpu.VMEM((64, 4096), BF),
            pltpu.VMEM((64, 512), BF),
            pltpu.VMEM((64, 512), BF),
            pltpu.VMEM((64, 4096), BF),
            pltpu.VMEM((64, 4096), BF),
            pltpu.VMEM((64, 512), BF),
            pltpu.VMEM((64, 512), BF),
            pltpu.VMEM((64, 4096), BF),
            pltpu.VMEM((1, 128), F32),
            pltpu.VMEM((1, 128), F32),
            pltpu.VMEM((1, 256), jnp.int32),
            pltpu.VMEM((1, N), jnp.int32),
            pltpu.VMEM((1, N), jnp.int32),
            pltpu.VMEM((1, N), jnp.int32),
            pltpu.SMEM((1, 256), jnp.int32),
            pltpu.SMEM((1, N), jnp.int32),
            pltpu.SMEM((1, N), jnp.int32),
            pltpu.SMEM((1, N), jnp.int32),
            pltpu.VMEM((1, 256), jnp.int32),
            pltpu.SemaphoreType.DMA((14,)),
            pltpu.SemaphoreType.DMA((4,)),
            pltpu.VMEM((128, 4096), BF),
            pltpu.VMEM((128, 512), BF),
            pltpu.VMEM((128, 512), BF),
            pltpu.VMEM((1, 128), F32),
            pltpu.VMEM((1, 128), F32),
            pltpu.SemaphoreType.DMA((11,)),
            pltpu.VMEM((4, 192, 512), BF),
            pltpu.VMEM((4, 192, 128), BF),
            pltpu.VMEM((64, 512), F32),
            pltpu.VMEM((64, 512), F32),
            pltpu.VMEM((2, 64, 512), BF),
            pltpu.VMEM((64, 1024), BF),
            pltpu.VMEM((N, 3, 16, 128), BF),
            pltpu.VMEM((N, 3, 16, 128), BF),
            pltpu.VMEM((256, 16, 128), BF),
            pltpu.VMEM((256, 16, 128), BF),
            pltpu.VMEM((NEAR, 3, 2, 16, 128), BF),
            pltpu.VMEM((NEAR, 3, 2, 16, 128), BF),
            pltpu.VMEM((N, 9, 16, 128), BF),
            pltpu.VMEM((N, 9, 16, 128), BF),
            pltpu.VMEM((NEAR, 2, 16, 128), BF),
            pltpu.VMEM((NEAR, 2, 16, 128), BF),
            pltpu.VMEM((NEAR, 2, 2, 16, 128), BF),
            pltpu.VMEM((NEAR, 2, 2, 16, 128), BF),
            pltpu.VMEM((N, 2, 16, 128), BF),
            pltpu.VMEM((N, 2, 16, 128), BF),
            pltpu.VMEM((1, 128), F32),
            pltpu.VMEM((N, 1, 128), F32),
            pltpu.VMEM((1, 128), F32),
            pltpu.VMEM((n_dp, 1, 128), F32),
            pltpu.VMEM((512, 256), BF),
            pltpu.VMEM((512, 512), BF),
            pltpu.VMEM((64, 512), F32),
            pltpu.VMEM((64, 512), F32),
            pltpu.VMEM((64, 512), F32),
            pltpu.SemaphoreType.DMA((8,)),
            pltpu.SemaphoreType.DMA((12,)),
            pltpu.SemaphoreType.DMA((2,)),
        ],
        compiler_params=pltpu.CompilerParams(
            collective_id=0, has_side_effects=True, vmem_limit_bytes=60 * 1024 * 1024
        ),
    )(
        pre_q, prefix_keys, prefix_values, pre_cot, gen_q, rollout_keys, rollout_values, gen_cot,
        q_gain.reshape(1, 128), k_gain.reshape(1, 128),
        piece_dest, prefix_parent, branch_parent, rewards,
    )
    results = (out_q, out_k, out_v, out_qg, out_kg)
    out_q, out_k, out_v, out_qg, out_kg = pl.pallas_call(
        write_out,
        out_shape=tuple(jax.ShapeDtypeStruct(x.shape, x.dtype) for x in results),
        in_specs=[hbm] * 5,
        out_specs=[hbm] * 5,
        scratch_shapes=[pltpu.VMEM(x.shape, x.dtype) for x in results]
        + [pltpu.SemaphoreType.DMA((8,)), pltpu.SemaphoreType.DMA((8,))],
    )(*results)
    return out_q, out_k, out_v, out_qg.reshape(128), out_kg.reshape(128)


def solution(mesh):
    rows = P(("dp", "ctx"), None)
    return jax.shard_map(
        body,
        mesh=mesh,
        in_specs=(rows,) * 8 + (P(), P()) + (P("dp", None),) * 4,
        out_specs=(rows, rows, rows, P(), P()),
        check_vma=False,
    )
```

```python
import math

import jax
import jax.numpy as jnp
from jax import lax
from jax.experimental import pallas as pl
from jax.experimental.pallas import tpu as pltpu
from jax.sharding import PartitionSpec as P

EPSILON = 1e-06
NZ, NY = 8, 4
N = NZ * NY
NEAR = N // 2
BF = jnp.bfloat16
F32 = jnp.float32
MESH = pl.DeviceIdType.MESH
SCALE = 1.0 / math.sqrt(128)


def iota(shape, axis):
    return lax.broadcasted_iota(jnp.int32, shape, axis)


def contract(a, b, da, db):
    return lax.dot_general(a, b, (((da,), (db,)), ((), ())), preferred_element_type=F32)


def inverse_norm(x):
    return lax.rsqrt(jnp.mean(x * x, axis=-1, keepdims=True) + EPSILON)


def norm_back(x, r, gain, upstream):
    scaled = gain * upstream
    inner = jnp.mean(x * scaled, axis=-1, keepdims=True)
    return r * scaled - x * (r * r * r) * inner


def attend_keys(q, cot, gain, keys, vals, mask):
    qn = (q * inverse_norm(q) * gain).astype(BF)
    weights = jnp.exp(contract(keys, qn, 1, 1) * SCALE) * mask
    probs = weights * (1.0 / jnp.sum(weights, axis=0, keepdims=True))
    dprob = contract(vals, cot, 1, 1)
    inner = jnp.sum(probs * dprob, axis=0, keepdims=True)
    dscore = (probs * (dprob - inner) * SCALE).astype(BF)
    return dscore, contract(dscore, qn, 1, 0), contract(probs.astype(BF), cot, 1, 0)


def attend_queries(q, gain, keys, dscore):
    return norm_back(q, inverse_norm(q), gain, contract(dscore, keys, 0, 0))


def kernel(*refs):
    ins, outs, rest = refs[:14], refs[14:19], refs[19:]
    held, small, (table, loaded, indexed) = rest[:14], rest[14:18], rest[18:21]
    compute(ins, outs, rest[21:26], held, small, table, loaded, indexed, *rest[26:])


def compute(
    ins, outs, staged, held, small, table, loaded, indexed,
    stored, dscores, allkeys, branch_x, dkb, pkv, rkv, s1a, r1a, s1b, r1b, s2a, r2a, s2b, r2b, t0, rt0, t12, rt12, s4, r4,
    g, rg, gd, rd, m0, m12, dkp, dvp, causal, send, recv, dsem,
):
    pre_q, pre_k, pre_v, pre_c, gen_q, gen_k, gen_v, gen_c, qg, kg, dest_row, pp_row, bp_row, rew_row = held
    inv_s, pp_s, bp_s, rew_s = small
    out_q, out_k, out_v, out_qg, out_kg = staged
    me = lax.axis_index("ctx")
    group = lax.axis_index("dp")
    n_dp = lax.axis_size("dp")

    def peer(k):
        j, m = lax.div(k, NY), lax.rem(k, NY)
        dz = NZ + NZ // 2 + lax.div(j + 1, 2) * (1 - 2 * lax.rem(j, 2))
        dy = NY + NY // 2 + lax.div(m + 1, 2) * (1 - 2 * lax.rem(m, 2))
        return lax.rem(lax.div(me, NY) + dz, NZ) * NY + lax.rem(me + dy, NY)

    def dp_peer(k):
        return lax.rem(group + k, n_dp)

    def copy(stage, src, dst, target):
        arrived = recv.at[8 + lax.div(me, 8)] if stage == 3 else recv.at[stage]
        return pltpu.make_async_remote_copy(
            src_ref=src, dst_ref=dst, send_sem=send.at[stage], recv_sem=arrived,
            device_id={"ctx": target}, device_id_type=MESH,
        )

    def await_all(sem, ref):
        pltpu.make_async_copy(ref, ref, sem).wait()

    def peers(body):
        @pl.loop(0, N - 1)
        def _(k):
            body(peer(k))

    def others(ref, size=1):
        return ref.at[pl.ds(0, (N - 1) * size)]

    def near_others(ref):
        return ref.at[pl.ds(0, NEAR - 1)]

    def near(j, dy, sign):
        dz = 2 - 4 * lax.rem(dy, 2) if j == 0 else (0, 1, -1, 0)[j]
        return lax.rem(lax.div(me, NY) + NZ + sign * dz, NZ) * NY + lax.rem(me + NY + sign * dy, NY)

    def store(i, output, rows):
        return pltpu.make_async_copy(staged[output].at[rows], outs[output].at[rows], stored.at[i])

    upper_half, lower_half = pl.ds(0, 64), pl.ds(64, 64)
    stores = [
        store(0, 0, upper_half), store(1, 1, lower_half), store(2, 2, lower_half),
        store(3, 1, upper_half), store(4, 2, upper_half), store(5, 3, pl.ds(0, 1)), store(6, 4, pl.ds(0, 1)),
    ]

    def store_branch(c):
        at = (lower_half, pl.ds(pl.multiple_of(1024 * c, 128), 1024))
        return pltpu.make_async_copy(staged[0].at[at], outs[0].at[at], stored.at[7 + c])

    barrier = pltpu.get_barrier_semaphore()

    def greet(t):
        pl.semaphore_signal(barrier, inc=1, device_id={"ctx": t}, device_id_type=MESH)

    peers(greet)

    @pl.loop(1, n_dp)
    def _(k):
        pl.semaphore_signal(barrier, inc=1, device_id={"dp": dp_peer(k)}, device_id_type=MESH)

    fetch = [pltpu.make_async_copy(ins[i], held[i], loaded.at[i]) for i in range(14)]
    fetch += [pltpu.make_async_copy(ins[i], small[i - 10], indexed.at[i - 10]) for i in (11, 12, 13)]
    for i in (9, 1, 2, 5, 6, 4, 7, 10, 11, 12, 13, 14, 15, 16, 8):
        fetch[i].start()
    for i in (9, 1, 2, 5, 6):
        fetch[i].wait()

    kgain = kg[...]

    for c in range(4):
        x = pre_k[:, c * 128:(c + 1) * 128].astype(F32)
        pkv[0, :, c * 128:(c + 1) * 128] = (x * inverse_norm(x) * kgain).astype(BF)
    pkv[1] = pre_v[...]
    rows = iota((64, 64), 0)
    spread = (8 * ((rows % 16) // 2) + 2 * (rows // 16) + rows % 2 == iota((64, 64), 1)).astype(F32).astype(BF)
    rkv[:, :512] = contract(spread, gen_k[...], 1, 0).astype(BF)
    rkv[:, 512:] = contract(spread, gen_v[...], 1, 0).astype(BF)

    for i in (4, 7):
        fetch[i].wait()
    pl.semaphore_wait(barrier, N - 1 + n_dp - 1)

    def fill_1a(t):
        rb = pl.multiple_of(lax.rem(lax.div(t, 4), 4) * 16, 16)
        cb = pl.multiple_of(lax.rem(t, 4) * 128, 128)
        s1a[t, 0:2] = pkv[:, pl.ds(rb, 16), pl.ds(cb, 128)]
        rp = pl.multiple_of(lax.rem(t, 4) * 16, 16)
        cr = pl.multiple_of((lax.div(t, 8) + 4 * lax.rem(lax.div(t, 4), 2)) * 128, 128)
        s1a[t, 2] = rkv[pl.ds(rp, 16), pl.ds(cr, 128)]

    def send_1a(t):
        fill_1a(t)
        copy(0, s1a.at[t], r1a.at[me], t).start()

    peers(send_1a)
    fill_1a(me)
    r1a[me] = s1a[me]

    def slab(t):
        cols = pl.ds(pl.multiple_of(t * 128, 128), 128)
        q = gen_q[:, cols].astype(F32).reshape(8, 8, 128)
        c = gen_c[:, cols].astype(F32).reshape(8, 8, 128)
        return jnp.concatenate([q, c], axis=1).astype(BF)

    def send_1b(t):
        part = s1b.at[pl.ds(t * 8, 8)]
        part[...] = slab(t)
        copy(1, part, r1b.at[pl.ds(me * 8, 8)], t).start()

    peers(send_1b)
    r1b[pl.ds(me * 8, 8)] = slab(me)

    for i in (8, 10, 11, 12, 13, 14, 15, 16):
        fetch[i].wait()
    qgain = qg[...]
    for i in (0, 3):
        fetch[i].start()
    column = jnp.broadcast_to(dest_row[...], (128, 256)).T
    for half in range(2):
        hit = column == iota((256, 128), 1) + 128 * half
        table[:, half * 128:(half + 1) * 128] = jnp.max(jnp.where(hit, iota((256, 128), 0), 0), axis=0, keepdims=True)
    lookup = pltpu.make_async_copy(table, inv_s, indexed.at[0])
    lookup.start()
    pp = jnp.broadcast_to(pp_row[...].astype(F32), (8, N))
    bp = jnp.broadcast_to(bp_row[...].astype(F32), (8, N))
    pick = (bp_row[...] == iota((N, N), 0)).astype(F32).astype(BF)
    upper = contract(pp.astype(BF), pick, 1, 0)
    def clients(lane, each):
        k = lane // each
        j, dy = k // NY, k % NY
        dz = jnp.where(j == 0, 2 - 4 * (dy % 2), jnp.where(j == 1, 1, jnp.where(j == 2, -1, 0)))
        at = (lax.div(me, NY) + NZ + dz) % NZ * NY + (me + dy) % NY
        return (iota(lane.shape, 0) == at).astype(F32).astype(BF)

    lane0, lane1 = iota((N, 256), 1), iota((N, 512), 1)
    id0 = contract(pp.astype(BF), clients(lane0, 16), 1, 0) * 16.0 + (lane0 % 16).astype(F32)[:8]
    spread1 = clients(lane1, 32)
    parent1 = contract(bp.astype(BF), spread1, 1, 0)
    upper1 = contract(upper.astype(BF), spread1, 1, 0)
    id1 = jnp.where(((lane1 // 16) % 2 == 0)[:8], parent1, upper1) * 16.0 + (lane1 % 16).astype(F32)[:8]
    m0[...] = (iota((512, 256), 0).astype(F32) == id0[:1]).astype(F32).astype(BF)
    m12[...] = (iota((512, 512), 0).astype(F32) == id1[:1]).astype(F32).astype(BF)
    dest = jnp.broadcast_to(dest_row[...].astype(F32), (8, 256)).astype(BF)
    spread2 = (iota((256, 512), 0) == iota((256, 512), 1) // 2).astype(F32).astype(BF)
    id2 = contract(dest, spread2, 1, 0) * 2.0 + (iota((8, 512), 1) % 2).astype(F32)
    order = (iota((512, 512), 0).astype(F32) == id2[:1]).astype(F32).astype(BF)
    causal[...] = (iota((64, 512), 0) <= iota((64, 512), 1) % 64).astype(F32)

    my_parent = bp_s[0, me]
    my_upper = pp_s[0, my_parent]
    my_above = pp_s[0, me]
    my_root = jnp.where(my_upper >= 0, my_upper, my_parent).astype(F32)
    root = jnp.where(upper >= 0.0, upper, bp)
    member = (root == my_root).astype(F32)
    score = jnp.broadcast_to(rew_row[...].astype(F32), (8, N))
    size = jnp.sum(member, axis=1, keepdims=True)
    center = jnp.sum(member * score, axis=1, keepdims=True) / size
    var = jnp.sum(member * (score - center) ** 2, axis=1, keepdims=True) / size
    adv = ((rew_s[0, me].astype(F32) - center) / jnp.maximum(jnp.sqrt(var), 1.0))[:1]

    await_all(recv.at[0], others(r1a))
    for j in range(4):
        for dy in (2, 1, 3, 0):
            t = near(j, dy, 1)
            k = 4 * j + dy
            parent = bp_s[0, t]
            s2a[k, 0] = r1a[jnp.maximum(pp_s[0, t], 0), 0:2]
            s2a[k, 1] = r1a[parent, 0:2]
            s2a[k, 2] = r1a[jnp.maximum(pp_s[0, parent], 0), 0:2]
            if k != 12:
                copy(2, s2a.at[k], r2a.at[lax.rem(me, NEAR)], t).start()
    r2a[lax.rem(me, NEAR)] = s2a[12]
    s2b[:, 8] = contract(order, r1a[:, 2].reshape(512, 128), 1, 0).astype(BF).reshape(N, 16, 128)

    lookup.wait()
    await_all(recv.at[1], others(r1b, 8))

    def send_2b(t):
        for p in range(8):
            s2b[t, p] = r1b[inv_s[0, t * 8 + p]]
        copy(3, s2b.at[t], r2b.at[me], t).start()

    peers(send_2b)
    for p in range(8):
        r2b[me, p] = r1b[inv_s[0, me * 8 + p]]
    r2b[me, 8] = s2b[me, 8]

    def above_rows(slot, which, c):
        return jnp.concatenate([r2a[4 * b + c, slot, which] for b in range(4)], axis=0)

    def own_rows(first):
        return jnp.concatenate([r2b[first + b, 8] for b in range(4)], axis=0)

    for i in (0, 3):
        fetch[i].wait()
    await_all(recv.at[2], near_others(r2a))
    g[...] = jnp.zeros((1, 128), F32)
    above = (my_above >= 0).astype(F32)

    @pl.loop(0, 4)
    def _(c):
        col = lambda base, h: pl.ds(pl.multiple_of((base + h) * 128, 128), 128)
        q = jnp.concatenate([pre_q[:, col(8 * c, h)] for h in range(8)], axis=0).astype(F32)
        cot = jnp.concatenate([pre_c[:, col(8 * c, h)] for h in range(8)], axis=0)
        own_k = pkv[0, :, col(c, 0)]
        far_k = above_rows(0, 0, c)
        keys = jnp.concatenate([own_k, far_k], axis=0)
        vals = jnp.concatenate([pkv[1, :, col(c, 0)], above_rows(0, 1, c)], axis=0)
        mask = jnp.concatenate([causal[...], jnp.full((64, 512), 1.0, F32) * above], axis=0)
        dscore, dk, dv = attend_keys(q, cot, qgain, keys, vals, mask)
        dq = attend_queries(q, qgain, keys, dscore)
        for h in range(8):
            out_q[0:64, col(8 * c, h)] = dq[h * 64:(h + 1) * 64].astype(BF)
        dkp[:, col(c, 0)] = dk[:64]
        dvp[:, col(c, 0)] = dv[:64]
        g[...] += jnp.sum(dk * keys.astype(F32), axis=0, keepdims=True)
        for b in range(4):
            t0[4 * b + c, 0] = dk[64 + 16 * b:80 + 16 * b].astype(BF)
            t0[4 * b + c, 1] = dv[64 + 16 * b:80 + 16 * b].astype(BF)

    stores[0].start()
    for j in range(4):
        for dy in (2, 1, 3, 0):
            t = near(j, dy, -1)
            if 4 * j + dy != 12:
                copy(4, t0.at[lax.rem(t, NEAR)], rt0.at[4 * j + dy], t).start()
    rt0[12] = t0[lax.rem(me, NEAR)]

    await_all(send.at[0], others(r1a))
    await_all(send.at[1], others(r1b, 8))
    await_all(send.at[2], near_others(r2a))

    back = (8 * ((iota((64, 64), 1) % 16) // 2) + 2 * (iota((64, 64), 1) // 16) + iota((64, 64), 1) % 2
            == iota((64, 64), 0)).astype(F32).astype(BF)
    upper_ok = (my_upper >= 0).astype(F32)

    @pl.loop(0, 4)
    def _(step):
        turn = (1 - 2 * lax.rem(step, 2)) * (1 - 2 * lax.rem(lax.div(me, NY), 2))
        c = lax.rem(lax.div(me, 8) + 6 + lax.div(step + 1, 2) * turn, 4)
        mine = c == lax.div(me, 8)

        @pl.when(mine)
        def _():
            await_all(recv.at[8 + c], r2b.at[pl.ds(0, 7)])

        @pl.when(jnp.logical_not(mine))
        def _():
            await_all(recv.at[8 + c], r2b.at[pl.ds(0, 8)])

        col = lambda base, h: pl.ds(pl.multiple_of((base + h) * 128, 128), 128)
        both = r2b[pl.ds(8 * c, 8), 0:8].reshape(64, 16, 128).astype(F32)
        q = both[:, :8].reshape(512, 128)
        cot = (both[:, 8:].reshape(512, 128) * adv).astype(BF)
        x = contract(back, own_rows(8 * c), 1, 0)
        r = inverse_norm(x)
        far_k = jnp.concatenate([above_rows(1, 0, c), above_rows(2, 0, c)], axis=0)
        keys = jnp.concatenate([(x * r * kgain).astype(BF), far_k], axis=0)
        vals = jnp.concatenate(
            [contract(back, own_rows(8 * c + 4), 1, 0).astype(BF), above_rows(1, 1, c), above_rows(2, 1, c)], axis=0
        )
        ones = jnp.full((64, 512), 1.0, F32)
        mask = jnp.concatenate([causal[...], ones, ones * upper_ok], axis=0)
        dscore, dk, dv = attend_keys(q, cot, qgain, keys, vals, mask)
        for b in range(4):
            for j in range(2):
                at = 64 + 64 * j + 16 * b
                t12[4 * b + c, j, 0] = dk[at:at + 16].astype(BF)
                t12[4 * b + c, j, 1] = dv[at:at + 16].astype(BF)
        dy = lax.rem(me + 4 - c, NY)
        for j in range(4):
            t = near(j, dy, -1)

            @pl.when(t != me)
            def _():
                copy(5, t12.at[lax.rem(t, NEAR)], rt12.at[4 * j + dy], t).start()

        out_v[64:128, col(c, 0)] = dv[:64].astype(BF)
        dscores[c] = dscore
        allkeys[c] = keys
        branch_x[:, col(c, 0)] = x
        dkb[:, col(c, 0)] = dk[:64]
        g[...] += jnp.sum(dk * keys.astype(F32), axis=0, keepdims=True)

    rt12[12] = t12[lax.rem(me, NEAR)]

    peers(lambda t: copy(6, g, rg.at[me], t).start())
    rg[me] = g[...]

    @pl.loop(0, 4)
    def _(c):
        col = lambda base, h: pl.ds(pl.multiple_of((base + h) * 128, 128), 128)
        q = r2b[pl.ds(8 * c, 8), 0:8].reshape(64, 16, 128).astype(F32)[:, :8].reshape(512, 128)
        dq = attend_queries(q, qgain, allkeys[c], dscores[c])
        for h in range(8):
            out_q[64:128, col(8 * c, h)] = dq[h * 64:(h + 1) * 64].astype(BF)
        store_branch(c).start()
        x, dk = branch_x[:, col(c, 0)], dkb[:, col(c, 0)]
        out_k[64:128, col(c, 0)] = norm_back(x, inverse_norm(x), kgain, dk).astype(BF)

    stores[1].start()
    stores[2].start()

    def columns(first, second, rows):
        return jnp.concatenate([first.reshape(rows, 128), second.reshape(rows, 128)], axis=1)

    await_all(recv.at[4], near_others(rt0))
    total = contract(m0[...], columns(rt0[:, 0], rt0[:, 1], 256), 1, 0)
    await_all(send.at[3], others(r2b))
    await_all(send.at[4], near_others(rt0))
    await_all(recv.at[5], near_others(rt12))
    total += contract(m12[...], columns(rt12[:, :, 0], rt12[:, :, 1], 512), 1, 0)
    s4[:, 0] = total[:, :128].astype(BF).reshape(N, 16, 128)
    s4[:, 1] = total[:, 128:].astype(BF).reshape(N, 16, 128)

    @pl.loop(0, N)
    def _(t):
        @pl.when(t != me)
        def _():
            copy(7, s4.at[t], r4.at[me], t).start()

    r4[me] = s4[me]

    await_all(recv.at[6], others(rg))
    gd[...] = jnp.sum(rg[...], axis=0)

    def dp_copy(k):
        t = dp_peer(k)
        return pltpu.make_async_remote_copy(
            src_ref=gd, dst_ref=rd.at[group], send_sem=dsem.at[0], recv_sem=dsem.at[1],
            device_id={"dp": t}, device_id_type=MESH,
        )

    @pl.loop(1, n_dp)
    def _(k):
        dp_copy(k).start()

    rd[group] = gd[...]

    await_all(recv.at[7], others(r4))
    def far_rows(which, c):
        pairs = [r4[4 * b + c, which].astype(F32) + r4[NEAR + 4 * b + c, which].astype(F32) for b in range(4)]
        return jnp.concatenate(pairs, axis=0)

    for c in range(4):
        cols = slice(c * 128, (c + 1) * 128)
        x = pre_k[:, cols].astype(F32)
        dk = dkp[:, cols] + far_rows(0, c)
        out_k[0:64, cols] = norm_back(x, inverse_norm(x), kgain, dk).astype(BF)
        out_v[0:64, cols] = (dvp[:, cols] + far_rows(1, c)).astype(BF)

    stores[3].start()
    stores[4].start()

    await_all(dsem.at[1], rd.at[pl.ds(0, n_dp - 1)])

    sums = jnp.sum(rd[...], axis=0)
    out_qg[...] = sums / qgain
    out_kg[...] = sums / kgain
    stores[5].start()
    stores[6].start()

    await_all(send.at[5], near_others(rt12))
    await_all(send.at[6], others(rg))
    await_all(send.at[7], others(r4))
    await_all(dsem.at[0], rd.at[pl.ds(0, n_dp - 1)])
    for each in stores:
        each.wait()

    @pl.loop(0, 4)
    def _(c):
        store_branch(c).wait()


def write_out(*refs):
    src, dst, mid = refs[:5], refs[5:10], refs[10:15]
    loads, stores = refs[15:]
    chunks = [(0, pl.ds(32 * i, 32)) for i in range(4)] + [(1, pl.ds(0, 128)), (2, pl.ds(0, 128))]
    chunks += [(3, pl.ds(0, 1)), (4, pl.ds(0, 1))]
    load = [pltpu.make_async_copy(src[a].at[r], mid[a].at[r], loads.at[n]) for n, (a, r) in enumerate(chunks)]
    store = [pltpu.make_async_copy(mid[a].at[r], dst[a].at[r], stores.at[n]) for n, (a, r) in enumerate(chunks)]
    for each in load:
        each.start()
    for first, then in zip(load, store):
        first.wait()
        then.start()
    for each in store:
        each.wait()


def body(
    pre_q, prefix_keys, prefix_values, pre_cot, gen_q, rollout_keys, rollout_values, gen_cot,
    q_gain, k_gain, piece_dest, prefix_parent, branch_parent, rewards,
):
    n_dp = lax.axis_size("dp")
    hbm = pl.BlockSpec(memory_space=pl.ANY)
    out_q, out_k, out_v, out_qg, out_kg = pl.pallas_call(
        kernel,
        out_shape=(
            jax.ShapeDtypeStruct((128, 4096), BF),
            jax.ShapeDtypeStruct((128, 512), BF),
            jax.ShapeDtypeStruct((128, 512), BF),
            jax.ShapeDtypeStruct((1, 128), F32),
            jax.ShapeDtypeStruct((1, 128), F32),
        ),
        in_specs=[hbm] * 14,
        out_specs=[hbm] * 5,
        scratch_shapes=[
            pltpu.VMEM((64, 4096), BF),
            pltpu.VMEM((64, 512), BF),
            pltpu.VMEM((64, 512), BF),
            pltpu.VMEM((64, 4096), BF),
            pltpu.VMEM((64, 4096), BF),
            pltpu.VMEM((64, 512), BF),
            pltpu.VMEM((64, 512), BF),
            pltpu.VMEM((64, 4096), BF),
            pltpu.VMEM((1, 128), F32),
            pltpu.VMEM((1, 128), F32),
            pltpu.VMEM((1, 256), jnp.int32),
            pltpu.VMEM((1, N), jnp.int32),
            pltpu.VMEM((1, N), jnp.int32),
            pltpu.VMEM((1, N), jnp.int32),
            pltpu.SMEM((1, 256), jnp.int32),
            pltpu.SMEM((1, N), jnp.int32),
            pltpu.SMEM((1, N), jnp.int32),
            pltpu.SMEM((1, N), jnp.int32),
            pltpu.VMEM((1, 256), jnp.int32),
            pltpu.SemaphoreType.DMA((14,)),
            pltpu.SemaphoreType.DMA((4,)),
            pltpu.VMEM((128, 4096), BF),
            pltpu.VMEM((128, 512), BF),
            pltpu.VMEM((128, 512), BF),
            pltpu.VMEM((1, 128), F32),
            pltpu.VMEM((1, 128), F32),
            pltpu.SemaphoreType.DMA((11,)),
            pltpu.VMEM((4, 192, 512), BF),
            pltpu.VMEM((4, 192, 128), BF),
            pltpu.VMEM((64, 512), F32),
            pltpu.VMEM((64, 512), F32),
            pltpu.VMEM((2, 64, 512), BF),
            pltpu.VMEM((64, 1024), BF),
            pltpu.VMEM((N, 3, 16, 128), BF),
            pltpu.VMEM((N, 3, 16, 128), BF),
            pltpu.VMEM((256, 16, 128), BF),
            pltpu.VMEM((256, 16, 128), BF),
            pltpu.VMEM((NEAR, 3, 2, 16, 128), BF),
            pltpu.VMEM((NEAR, 3, 2, 16, 128), BF),
            pltpu.VMEM((N, 9, 16, 128), BF),
            pltpu.VMEM((N, 9, 16, 128), BF),
            pltpu.VMEM((NEAR, 2, 16, 128), BF),
            pltpu.VMEM((NEAR, 2, 16, 128), BF),
            pltpu.VMEM((NEAR, 2, 2, 16, 128), BF),
            pltpu.VMEM((NEAR, 2, 2, 16, 128), BF),
            pltpu.VMEM((N, 2, 16, 128), BF),
            pltpu.VMEM((N, 2, 16, 128), BF),
            pltpu.VMEM((1, 128), F32),
            pltpu.VMEM((N, 1, 128), F32),
            pltpu.VMEM((1, 128), F32),
            pltpu.VMEM((n_dp, 1, 128), F32),
            pltpu.VMEM((512, 256), BF),
            pltpu.VMEM((512, 512), BF),
            pltpu.VMEM((64, 512), F32),
            pltpu.VMEM((64, 512), F32),
            pltpu.VMEM((64, 512), F32),
            pltpu.SemaphoreType.DMA((8,)),
            pltpu.SemaphoreType.DMA((12,)),
            pltpu.SemaphoreType.DMA((2,)),
        ],
        compiler_params=pltpu.CompilerParams(
            collective_id=0, has_side_effects=True, vmem_limit_bytes=60 * 1024 * 1024
        ),
    )(
        pre_q, prefix_keys, prefix_values, pre_cot, gen_q, rollout_keys, rollout_values, gen_cot,
        q_gain.reshape(1, 128), k_gain.reshape(1, 128),
        piece_dest, prefix_parent, branch_parent, rewards,
    )
    results = (out_q, out_k, out_v, out_qg, out_kg)
    out_q, out_k, out_v, out_qg, out_kg = pl.pallas_call(
        write_out,
        out_shape=tuple(jax.ShapeDtypeStruct(x.shape, x.dtype) for x in results),
        in_specs=[hbm] * 5,
        out_specs=[hbm] * 5,
        scratch_shapes=[pltpu.VMEM(x.shape, x.dtype) for x in results]
        + [pltpu.SemaphoreType.DMA((8,)), pltpu.SemaphoreType.DMA((8,))],
    )(*results)
    return out_q, out_k, out_v, out_qg.reshape(128), out_kg.reshape(128)


def solution(mesh):
    rows = P(("dp", "ctx"), None)
    return jax.shard_map(
        body,
        mesh=mesh,
        in_specs=(rows,) * 8 + (P(), P()) + (P("dp", None),) * 4,
        out_specs=(rows, rows, rows, P(), P()),
        check_vma=False,
    )
```

```python
import math

import jax
import jax.numpy as jnp
from jax import lax
from jax.experimental import pallas as pl
from jax.experimental.pallas import tpu as pltpu
from jax.sharding import PartitionSpec as P

EPSILON = 1e-06
NZ, NY = 8, 4
N = NZ * NY
NEAR = N // 2
BF = jnp.bfloat16
F32 = jnp.float32
MESH = pl.DeviceIdType.MESH
SCALE = 1.0 / math.sqrt(128)


def iota(shape, axis):
    return lax.broadcasted_iota(jnp.int32, shape, axis)


def contract(a, b, da, db):
    return lax.dot_general(a, b, (((da,), (db,)), ((), ())), preferred_element_type=F32)


def inverse_norm(x):
    return lax.rsqrt(jnp.mean(x * x, axis=-1, keepdims=True) + EPSILON)


def norm_back(x, r, gain, upstream):
    scaled = gain * upstream
    inner = jnp.mean(x * scaled, axis=-1, keepdims=True)
    return r * scaled - x * (r * r * r) * inner


def attend_keys(q, cot, gain, keys, vals, causal, last):
    qn = (q * inverse_norm(q) * gain).astype(BF)
    raw = jnp.exp(contract(keys, qn, 1, 1) * SCALE)
    middle = [raw[64:128]] if keys.shape[0] == 192 else []
    weights = jnp.concatenate([raw[:64] * causal, *middle, raw[-64:] * last], axis=0)
    probs = weights * (1.0 / jnp.sum(weights, axis=0, keepdims=True))
    dprob = contract(vals, cot, 1, 1)
    inner = jnp.sum(probs * dprob, axis=0, keepdims=True)
    dscore = (probs * (dprob - inner) * SCALE).astype(BF)
    return dscore, contract(dscore, qn, 1, 0), contract(probs.astype(BF), cot, 1, 0)


def attend_queries(q, gain, keys, dscore):
    return norm_back(q, inverse_norm(q), gain, contract(dscore, keys, 0, 0))


def kernel(*refs):
    ins, outs, rest = refs[:14], refs[14:19], refs[19:]
    held, small, (table, loaded, indexed) = rest[:14], rest[14:18], rest[18:21]
    compute(ins, outs, rest[21:26], held, small, table, loaded, indexed, *rest[26:])


def compute(
    ins, outs, staged, held, small, table, loaded, indexed,
    stored, dscores, allkeys, branch_x, dkb, pkv, rkv, s1a, r1a, s1b, r1b, s2a, r2a, s2b, r2b, t0, rt0, t12, rt12, s4, r4,
    g, rg, gd, rd, m0, m12, dkp, dvp, causal, send, recv, dsem,
):
    pre_q, pre_k, pre_v, pre_c, gen_q, gen_k, gen_v, gen_c, qg, kg, dest_row, pp_row, bp_row, rew_row = held
    inv_s, pp_s, bp_s, rew_s = small
    out_q, out_k, out_v, out_qg, out_kg = staged
    me = lax.axis_index("ctx")
    group = lax.axis_index("dp")
    n_dp = lax.axis_size("dp")

    def peer(k):
        j, m = lax.div(k, NY), lax.rem(k, NY)
        dz = NZ + NZ // 2 + lax.div(j + 1, 2) * (1 - 2 * lax.rem(j, 2))
        dy = NY + NY // 2 + lax.div(m + 1, 2) * (1 - 2 * lax.rem(m, 2))
        return lax.rem(lax.div(me, NY) + dz, NZ) * NY + lax.rem(me + dy, NY)

    def dp_peer(k):
        return lax.rem(group + k, n_dp)

    def copy(stage, src, dst, target):
        arrived = recv.at[8 + lax.div(me, 8)] if stage == 3 else recv.at[stage]
        return pltpu.make_async_remote_copy(
            src_ref=src, dst_ref=dst, send_sem=send.at[stage], recv_sem=arrived,
            device_id={"ctx": target}, device_id_type=MESH,
        )

    def await_all(sem, ref):
        pltpu.make_async_copy(ref, ref, sem).wait()

    def peers(body):
        @pl.loop(0, N - 1)
        def _(k):
            body(peer(k))

    def others(ref, size=1):
        return ref.at[pl.ds(0, (N - 1) * size)]

    def near_others(ref):
        return ref.at[pl.ds(0, NEAR - 1)]

    def near(j, dy, sign):
        dz = 2 - 4 * lax.rem(dy, 2) if j == 0 else (0, 1, -1, 0)[j]
        return lax.rem(lax.div(me, NY) + NZ + sign * dz, NZ) * NY + lax.rem(me + NY + sign * dy, NY)

    def store(i, output, rows):
        return pltpu.make_async_copy(staged[output].at[rows], outs[output].at[rows], stored.at[i])

    upper_half, lower_half = pl.ds(0, 64), pl.ds(64, 64)
    stores = [
        store(0, 0, upper_half), store(1, 1, lower_half), store(2, 2, lower_half),
        store(3, 1, upper_half), store(4, 2, upper_half), store(5, 3, pl.ds(0, 1)), store(6, 4, pl.ds(0, 1)),
    ]

    def store_branch(c):
        at = (lower_half, pl.ds(pl.multiple_of(1024 * c, 128), 1024))
        return pltpu.make_async_copy(staged[0].at[at], outs[0].at[at], stored.at[7 + c])

    barrier = pltpu.get_barrier_semaphore()

    def greet(t):
        pl.semaphore_signal(barrier, inc=1, device_id={"ctx": t}, device_id_type=MESH)

    peers(greet)

    @pl.loop(1, n_dp)
    def _(k):
        pl.semaphore_signal(barrier, inc=1, device_id={"dp": dp_peer(k)}, device_id_type=MESH)

    fetch = [pltpu.make_async_copy(ins[i], held[i], loaded.at[i]) for i in range(14)]
    fetch += [pltpu.make_async_copy(ins[i], small[i - 10], indexed.at[i - 10]) for i in (11, 12, 13)]
    for i in (9, 1, 2, 5, 6, 4, 7, 10, 11, 12, 13, 14, 15, 16, 8):
        fetch[i].start()
    for i in (9, 1, 2, 5, 6):
        fetch[i].wait()

    kgain = kg[...]

    for c in range(4):
        x = pre_k[:, c * 128:(c + 1) * 128].astype(F32)
        pkv[0, :, c * 128:(c + 1) * 128] = (x * inverse_norm(x) * kgain).astype(BF)
    pkv[1] = pre_v[...]
    rows = iota((64, 64), 0)
    spread = (8 * ((rows % 16) // 2) + 2 * (rows // 16) + rows % 2 == iota((64, 64), 1)).astype(F32).astype(BF)
    rkv[:, :512] = contract(spread, gen_k[...], 1, 0).astype(BF)
    rkv[:, 512:] = contract(spread, gen_v[...], 1, 0).astype(BF)

    for i in (4, 7):
        fetch[i].wait()
    pl.semaphore_wait(barrier, N - 1 + n_dp - 1)

    def fill_1a(t):
        rb = pl.multiple_of(lax.rem(lax.div(t, 4), 4) * 16, 16)
        cb = pl.multiple_of(lax.rem(t, 4) * 128, 128)
        s1a[t, 0:2] = pkv[:, pl.ds(rb, 16), pl.ds(cb, 128)]
        rp = pl.multiple_of(lax.rem(t, 4) * 16, 16)
        cr = pl.multiple_of((lax.div(t, 8) + 4 * lax.rem(lax.div(t, 4), 2)) * 128, 128)
        s1a[t, 2] = rkv[pl.ds(rp, 16), pl.ds(cr, 128)]

    def send_1a(t):
        fill_1a(t)
        copy(0, s1a.at[t], r1a.at[me], t).start()

    peers(send_1a)
    fill_1a(me)
    r1a[me] = s1a[me]

    def slab(t):
        cols = pl.ds(pl.multiple_of(t * 128, 128), 128)
        q = gen_q[:, cols].astype(F32).reshape(8, 8, 128)
        c = gen_c[:, cols].astype(F32).reshape(8, 8, 128)
        return jnp.concatenate([q, c], axis=1).astype(BF)

    def send_1b(t):
        part = s1b.at[pl.ds(t * 8, 8)]
        part[...] = slab(t)
        copy(1, part, r1b.at[pl.ds(me * 8, 8)], t).start()

    peers(send_1b)
    r1b[pl.ds(me * 8, 8)] = slab(me)

    for i in (8, 10, 11, 12, 13, 14, 15, 16):
        fetch[i].wait()
    qgain = qg[...]
    for i in (0, 3):
        fetch[i].start()
    column = jnp.broadcast_to(dest_row[...], (128, 256)).T
    for half in range(2):
        hit = column == iota((256, 128), 1) + 128 * half
        table[:, half * 128:(half + 1) * 128] = jnp.max(jnp.where(hit, iota((256, 128), 0), 0), axis=0, keepdims=True)
    lookup = pltpu.make_async_copy(table, inv_s, indexed.at[0])
    lookup.start()
    pp = jnp.broadcast_to(pp_row[...].astype(F32), (8, N))
    bp = jnp.broadcast_to(bp_row[...].astype(F32), (8, N))
    pick = (bp_row[...] == iota((N, N), 0)).astype(F32).astype(BF)
    upper = contract(pp.astype(BF), pick, 1, 0)
    def clients(lane, each):
        k = lane // each
        j, dy = k // NY, k % NY
        dz = jnp.where(j == 0, 2 - 4 * (dy % 2), jnp.where(j == 1, 1, jnp.where(j == 2, -1, 0)))
        at = (lax.div(me, NY) + NZ + dz) % NZ * NY + (me + dy) % NY
        return (iota(lane.shape, 0) == at).astype(F32).astype(BF)

    lane0, lane1 = iota((N, 256), 1), iota((N, 512), 1)
    id0 = contract(pp.astype(BF), clients(lane0, 16), 1, 0) * 16.0 + (lane0 % 16).astype(F32)[:8]
    spread1 = clients(lane1, 32)
    parent1 = contract(bp.astype(BF), spread1, 1, 0)
    upper1 = contract(upper.astype(BF), spread1, 1, 0)
    id1 = jnp.where(((lane1 // 16) % 2 == 0)[:8], parent1, upper1) * 16.0 + (lane1 % 16).astype(F32)[:8]
    m0[...] = (iota((512, 256), 0).astype(F32) == id0[:1]).astype(F32).astype(BF)
    m12[...] = (iota((512, 512), 0).astype(F32) == id1[:1]).astype(F32).astype(BF)
    dest = jnp.broadcast_to(dest_row[...].astype(F32), (8, 256)).astype(BF)
    spread2 = (iota((256, 512), 0) == iota((256, 512), 1) // 2).astype(F32).astype(BF)
    id2 = contract(dest, spread2, 1, 0) * 2.0 + (iota((8, 512), 1) % 2).astype(F32)
    order = (iota((512, 512), 0).astype(F32) == id2[:1]).astype(F32).astype(BF)
    causal[...] = (iota((64, 512), 0) <= iota((64, 512), 1) % 64).astype(F32)

    my_parent = bp_s[0, me]
    my_upper = pp_s[0, my_parent]
    my_above = pp_s[0, me]
    my_root = jnp.where(my_upper >= 0, my_upper, my_parent).astype(F32)
    root = jnp.where(upper >= 0.0, upper, bp)
    member = (root == my_root).astype(F32)
    score = jnp.broadcast_to(rew_row[...].astype(F32), (8, N))
    size = jnp.sum(member, axis=1, keepdims=True)
    center = jnp.sum(member * score, axis=1, keepdims=True) / size
    var = jnp.sum(member * (score - center) ** 2, axis=1, keepdims=True) / size
    adv = ((rew_s[0, me].astype(F32) - center) / jnp.maximum(jnp.sqrt(var), 1.0))[:1]

    await_all(recv.at[0], others(r1a))
    for j in range(4):
        for dy in (2, 1, 3, 0):
            t = near(j, dy, 1)
            k = 4 * j + dy
            parent = bp_s[0, t]
            s2a[k, 0] = r1a[jnp.maximum(pp_s[0, t], 0), 0:2]
            s2a[k, 1] = r1a[parent, 0:2]
            s2a[k, 2] = r1a[jnp.maximum(pp_s[0, parent], 0), 0:2]
            if k != 12:
                copy(2, s2a.at[k], r2a.at[lax.rem(me, NEAR)], t).start()
    r2a[lax.rem(me, NEAR)] = s2a[12]
    s2b[:, 8] = contract(order, r1a[:, 2].reshape(512, 128), 1, 0).astype(BF).reshape(N, 16, 128)

    lookup.wait()
    await_all(recv.at[1], others(r1b, 8))

    def send_2b(t):
        for p in range(8):
            s2b[t, p] = r1b[inv_s[0, t * 8 + p]]
        copy(3, s2b.at[t], r2b.at[me], t).start()

    peers(send_2b)
    for p in range(8):
        r2b[me, p] = r1b[inv_s[0, me * 8 + p]]
    r2b[me, 8] = s2b[me, 8]

    def above_rows(slot, which, c):
        return jnp.concatenate([r2a[4 * b + c, slot, which] for b in range(4)], axis=0)

    def own_rows(first):
        return jnp.concatenate([r2b[first + b, 8] for b in range(4)], axis=0)

    for i in (0, 3):
        fetch[i].wait()
    await_all(recv.at[2], near_others(r2a))
    g[...] = jnp.zeros((1, 128), F32)
    above = (my_above >= 0).astype(F32)

    @pl.loop(0, 4)
    def _(c):
        col = lambda base, h: pl.ds(pl.multiple_of((base + h) * 128, 128), 128)
        q = jnp.concatenate([pre_q[:, col(8 * c, h)] for h in range(8)], axis=0).astype(F32)
        cot = jnp.concatenate([pre_c[:, col(8 * c, h)] for h in range(8)], axis=0)
        own_k = pkv[0, :, col(c, 0)]
        far_k = above_rows(0, 0, c)
        keys = jnp.concatenate([own_k, far_k], axis=0)
        vals = jnp.concatenate([pkv[1, :, col(c, 0)], above_rows(0, 1, c)], axis=0)
        dscore, dk, dv = attend_keys(q, cot, qgain, keys, vals, causal[...], above)
        dq = attend_queries(q, qgain, keys, dscore)
        for h in range(8):
            out_q[0:64, col(8 * c, h)] = dq[h * 64:(h + 1) * 64].astype(BF)
        dkp[:, col(c, 0)] = dk[:64]
        dvp[:, col(c, 0)] = dv[:64]
        g[...] += jnp.sum(dk * keys.astype(F32), axis=0, keepdims=True)
        for b in range(4):
            t0[4 * b + c, 0] = dk[64 + 16 * b:80 + 16 * b].astype(BF)
            t0[4 * b + c, 1] = dv[64 + 16 * b:80 + 16 * b].astype(BF)

    stores[0].start()
    for j in range(4):
        for dy in (2, 1, 3, 0):
            t = near(j, dy, -1)
            if 4 * j + dy != 12:
                copy(4, t0.at[lax.rem(t, NEAR)], rt0.at[4 * j + dy], t).start()
    rt0[12] = t0[lax.rem(me, NEAR)]

    await_all(send.at[0], others(r1a))
    await_all(send.at[1], others(r1b, 8))
    await_all(send.at[2], near_others(r2a))

    back = (8 * ((iota((64, 64), 1) % 16) // 2) + 2 * (iota((64, 64), 1) // 16) + iota((64, 64), 1) % 2
            == iota((64, 64), 0)).astype(F32).astype(BF)
    upper_ok = (my_upper >= 0).astype(F32)

    @pl.loop(0, 4)
    def _(step):
        turn = (1 - 2 * lax.rem(step, 2)) * (1 - 2 * lax.rem(lax.div(me, NY), 2))
        c = lax.rem(lax.div(me, 8) + 6 + lax.div(step + 1, 2) * turn, 4)
        mine = c == lax.div(me, 8)

        @pl.when(mine)
        def _():
            await_all(recv.at[8 + c], r2b.at[pl.ds(0, 7)])

        @pl.when(jnp.logical_not(mine))
        def _():
            await_all(recv.at[8 + c], r2b.at[pl.ds(0, 8)])

        col = lambda base, h: pl.ds(pl.multiple_of((base + h) * 128, 128), 128)
        both = r2b[pl.ds(8 * c, 8), 0:8].reshape(64, 16, 128).astype(F32)
        q = both[:, :8].reshape(512, 128)
        cot = (both[:, 8:].reshape(512, 128) * adv).astype(BF)
        x = contract(back, own_rows(8 * c), 1, 0)
        r = inverse_norm(x)
        far_k = jnp.concatenate([above_rows(1, 0, c), above_rows(2, 0, c)], axis=0)
        keys = jnp.concatenate([(x * r * kgain).astype(BF), far_k], axis=0)
        vals = jnp.concatenate(
            [contract(back, own_rows(8 * c + 4), 1, 0).astype(BF), above_rows(1, 1, c), above_rows(2, 1, c)], axis=0
        )
        dscore, dk, dv = attend_keys(q, cot, qgain, keys, vals, causal[...], upper_ok)
        for b in range(4):
            for j in range(2):
                at = 64 + 64 * j + 16 * b
                t12[4 * b + c, j, 0] = dk[at:at + 16].astype(BF)
                t12[4 * b + c, j, 1] = dv[at:at + 16].astype(BF)
        dy = lax.rem(me + 4 - c, NY)
        for j in range(4):
            t = near(j, dy, -1)

            @pl.when(t != me)
            def _():
                copy(5, t12.at[lax.rem(t, NEAR)], rt12.at[4 * j + dy], t).start()

        out_v[64:128, col(c, 0)] = dv[:64].astype(BF)
        dscores[c] = dscore
        allkeys[c] = keys
        branch_x[:, col(c, 0)] = x
        dkb[:, col(c, 0)] = dk[:64]
        g[...] += jnp.sum(dk * keys.astype(F32), axis=0, keepdims=True)

    rt12[12] = t12[lax.rem(me, NEAR)]

    peers(lambda t: copy(6, g, rg.at[me], t).start())
    rg[me] = g[...]

    @pl.loop(0, 4)
    def _(c):
        col = lambda base, h: pl.ds(pl.multiple_of((base + h) * 128, 128), 128)
        q = r2b[pl.ds(8 * c, 8), 0:8].reshape(64, 16, 128).astype(F32)[:, :8].reshape(512, 128)
        dq = attend_queries(q, qgain, allkeys[c], dscores[c])
        for h in range(8):
            out_q[64:128, col(8 * c, h)] = dq[h * 64:(h + 1) * 64].astype(BF)
        store_branch(c).start()
        x, dk = branch_x[:, col(c, 0)], dkb[:, col(c, 0)]
        out_k[64:128, col(c, 0)] = norm_back(x, inverse_norm(x), kgain, dk).astype(BF)

    stores[1].start()
    stores[2].start()

    def columns(first, second, rows):
        return jnp.concatenate([first.reshape(rows, 128), second.reshape(rows, 128)], axis=1)

    await_all(recv.at[4], near_others(rt0))
    total = contract(m0[...], columns(rt0[:, 0], rt0[:, 1], 256), 1, 0)
    await_all(send.at[3], others(r2b))
    await_all(send.at[4], near_others(rt0))
    await_all(recv.at[5], near_others(rt12))
    total += contract(m12[...], columns(rt12[:, :, 0], rt12[:, :, 1], 512), 1, 0)
    s4[:, 0] = total[:, :128].astype(BF).reshape(N, 16, 128)
    s4[:, 1] = total[:, 128:].astype(BF).reshape(N, 16, 128)

    @pl.loop(0, N)
    def _(t):
        @pl.when(t != me)
        def _():
            copy(7, s4.at[t], r4.at[me], t).start()

    r4[me] = s4[me]

    await_all(recv.at[6], others(rg))
    gd[...] = jnp.sum(rg[...], axis=0)

    def dp_copy(k):
        t = dp_peer(k)
        return pltpu.make_async_remote_copy(
            src_ref=gd, dst_ref=rd.at[group], send_sem=dsem.at[0], recv_sem=dsem.at[1],
            device_id={"dp": t}, device_id_type=MESH,
        )

    @pl.loop(1, n_dp)
    def _(k):
        dp_copy(k).start()

    rd[group] = gd[...]

    xs = [pre_k[:, c * 128:(c + 1) * 128].astype(F32) for c in range(4)]
    rs = [inverse_norm(x) for x in xs]
    await_all(send.at[5], near_others(rt12))
    await_all(send.at[6], others(rg))

    def far_rows(which, c):
        pairs = [r4[4 * b + c, which].astype(F32) + r4[NEAR + 4 * b + c, which].astype(F32) for b in range(4)]
        return jnp.concatenate(pairs, axis=0)

    await_all(recv.at[7], others(r4))
    for c in range(4):
        cols = slice(c * 128, (c + 1) * 128)
        out_v[0:64, cols] = (dvp[:, cols] + far_rows(1, c)).astype(BF)
    stores[4].start()
    for c in range(4):
        cols = slice(c * 128, (c + 1) * 128)
        out_k[0:64, cols] = norm_back(xs[c], rs[c], kgain, dkp[:, cols] + far_rows(0, c)).astype(BF)
    stores[3].start()

    await_all(dsem.at[1], rd.at[pl.ds(0, n_dp - 1)])

    sums = jnp.sum(rd[...], axis=0)
    out_qg[...] = sums / qgain
    out_kg[...] = sums / kgain
    stores[5].start()
    stores[6].start()

    await_all(send.at[7], others(r4))
    await_all(dsem.at[0], rd.at[pl.ds(0, n_dp - 1)])
    for each in stores:
        each.wait()

    @pl.loop(0, 4)
    def _(c):
        store_branch(c).wait()


def write_out(*refs):
    src, dst, mid = refs[:5], refs[5:10], refs[10:15]
    loads, stores = refs[15:]
    chunks = [(0, pl.ds(32 * i, 32)) for i in range(4)] + [(1, pl.ds(0, 128)), (2, pl.ds(0, 128))]
    chunks += [(3, pl.ds(0, 1)), (4, pl.ds(0, 1))]
    load = [pltpu.make_async_copy(src[a].at[r], mid[a].at[r], loads.at[n]) for n, (a, r) in enumerate(chunks)]
    store = [pltpu.make_async_copy(mid[a].at[r], dst[a].at[r], stores.at[n]) for n, (a, r) in enumerate(chunks)]
    for each in load:
        each.start()
    for first, then in zip(load, store):
        first.wait()
        then.start()
    for each in store:
        each.wait()


def body(
    pre_q, prefix_keys, prefix_values, pre_cot, gen_q, rollout_keys, rollout_values, gen_cot,
    q_gain, k_gain, piece_dest, prefix_parent, branch_parent, rewards,
):
    n_dp = lax.axis_size("dp")
    hbm = pl.BlockSpec(memory_space=pl.ANY)
    out_q, out_k, out_v, out_qg, out_kg = pl.pallas_call(
        kernel,
        out_shape=(
            jax.ShapeDtypeStruct((128, 4096), BF),
            jax.ShapeDtypeStruct((128, 512), BF),
            jax.ShapeDtypeStruct((128, 512), BF),
            jax.ShapeDtypeStruct((1, 128), F32),
            jax.ShapeDtypeStruct((1, 128), F32),
        ),
        in_specs=[hbm] * 14,
        out_specs=[hbm] * 5,
        scratch_shapes=[
            pltpu.VMEM((64, 4096), BF),
            pltpu.VMEM((64, 512), BF),
            pltpu.VMEM((64, 512), BF),
            pltpu.VMEM((64, 4096), BF),
            pltpu.VMEM((64, 4096), BF),
            pltpu.VMEM((64, 512), BF),
            pltpu.VMEM((64, 512), BF),
            pltpu.VMEM((64, 4096), BF),
            pltpu.VMEM((1, 128), F32),
            pltpu.VMEM((1, 128), F32),
            pltpu.VMEM((1, 256), jnp.int32),
            pltpu.VMEM((1, N), jnp.int32),
            pltpu.VMEM((1, N), jnp.int32),
            pltpu.VMEM((1, N), jnp.int32),
            pltpu.SMEM((1, 256), jnp.int32),
            pltpu.SMEM((1, N), jnp.int32),
            pltpu.SMEM((1, N), jnp.int32),
            pltpu.SMEM((1, N), jnp.int32),
            pltpu.VMEM((1, 256), jnp.int32),
            pltpu.SemaphoreType.DMA((14,)),
            pltpu.SemaphoreType.DMA((4,)),
            pltpu.VMEM((128, 4096), BF),
            pltpu.VMEM((128, 512), BF),
            pltpu.VMEM((128, 512), BF),
            pltpu.VMEM((1, 128), F32),
            pltpu.VMEM((1, 128), F32),
            pltpu.SemaphoreType.DMA((11,)),
            pltpu.VMEM((4, 192, 512), BF),
            pltpu.VMEM((4, 192, 128), BF),
            pltpu.VMEM((64, 512), F32),
            pltpu.VMEM((64, 512), F32),
            pltpu.VMEM((2, 64, 512), BF),
            pltpu.VMEM((64, 1024), BF),
            pltpu.VMEM((N, 3, 16, 128), BF),
            pltpu.VMEM((N, 3, 16, 128), BF),
            pltpu.VMEM((256, 16, 128), BF),
            pltpu.VMEM((256, 16, 128), BF),
            pltpu.VMEM((NEAR, 3, 2, 16, 128), BF),
            pltpu.VMEM((NEAR, 3, 2, 16, 128), BF),
            pltpu.VMEM((N, 9, 16, 128), BF),
            pltpu.VMEM((N, 9, 16, 128), BF),
            pltpu.VMEM((NEAR, 2, 16, 128), BF),
            pltpu.VMEM((NEAR, 2, 16, 128), BF),
            pltpu.VMEM((NEAR, 2, 2, 16, 128), BF),
            pltpu.VMEM((NEAR, 2, 2, 16, 128), BF),
            pltpu.VMEM((N, 2, 16, 128), BF),
            pltpu.VMEM((N, 2, 16, 128), BF),
            pltpu.VMEM((1, 128), F32),
            pltpu.VMEM((N, 1, 128), F32),
            pltpu.VMEM((1, 128), F32),
            pltpu.VMEM((n_dp, 1, 128), F32),
            pltpu.VMEM((512, 256), BF),
            pltpu.VMEM((512, 512), BF),
            pltpu.VMEM((64, 512), F32),
            pltpu.VMEM((64, 512), F32),
            pltpu.VMEM((64, 512), F32),
            pltpu.SemaphoreType.DMA((8,)),
            pltpu.SemaphoreType.DMA((12,)),
            pltpu.SemaphoreType.DMA((2,)),
        ],
        compiler_params=pltpu.CompilerParams(
            collective_id=0, has_side_effects=True, vmem_limit_bytes=60 * 1024 * 1024
        ),
    )(
        pre_q, prefix_keys, prefix_values, pre_cot, gen_q, rollout_keys, rollout_values, gen_cot,
        q_gain.reshape(1, 128), k_gain.reshape(1, 128),
        piece_dest, prefix_parent, branch_parent, rewards,
    )
    results = (out_q, out_k, out_v, out_qg, out_kg)
    out_q, out_k, out_v, out_qg, out_kg = pl.pallas_call(
        write_out,
        out_shape=tuple(jax.ShapeDtypeStruct(x.shape, x.dtype) for x in results),
        in_specs=[hbm] * 5,
        out_specs=[hbm] * 5,
        scratch_shapes=[pltpu.VMEM(x.shape, x.dtype) for x in results]
        + [pltpu.SemaphoreType.DMA((8,)), pltpu.SemaphoreType.DMA((8,))],
    )(*results)
    return out_q, out_k, out_v, out_qg.reshape(128), out_kg.reshape(128)


def solution(mesh):
    rows = P(("dp", "ctx"), None)
    return jax.shard_map(
        body,
        mesh=mesh,
        in_specs=(rows,) * 8 + (P(), P()) + (P("dp", None),) * 4,
        out_specs=(rows, rows, rows, P(), P()),
        check_vma=False,
    )
```
